32 devices in a mesh: dp: 2 (over x), expert: 16 (over z, y, core).
Axes of the slice: x: 2, y: 2, z: 4, core: 2. Of those that a mesh axis runs over, the one named last changes fastest.
Arguments:
- grad_out: bfloat16 [2048, 4096], P('expert', 'dp'), may hold values from -6 to 6
- routing: int32 [2048, 6], P('expert'), may hold values from 0 to 15, all different within a row; in each aligned block of 128 rows (0 to 127, 128 to 255, ...) at most 56 rows name the same one
- gates: float32 [2048, 6], P('expert'), may hold values from 0.05 to 1
- scales: float32 [2048], P('expert'), may hold values from 0.25 to 4
- saved_gate: bfloat16 [16, 1408, 896], P('expert'), may hold values from -6 to 6
- saved_up: bfloat16 [16, 1408, 896], P('expert'), may hold values from -6 to 6
- w_gate: bfloat16 [16, 4096, 1408], P('expert', 'dp'), may hold values from -0.09375 to 0.09375
- w_up: bfloat16 [16, 4096, 1408], P('expert', 'dp'), may hold values from -0.09375 to 0.09375
- w_down: bfloat16 [16, 1408, 4096], P('expert', None, 'dp'), may hold values from -0.15625 to 0.15625
Outputs:
- grad_x: bfloat16 [2048, 4096], P('expert', 'dp')
- grad_down: bfloat16 [16, 1408, 4096], P('expert', None, 'dp')
The draws below stay inside these ranges and needn't reach their ends.
Inputs may be any that keep to these rules, and one draw needn't show every extreme that they name: `routing`: each row names 6 different experts; within each token group of 128 rows no expert is named more than 56 times, a bound that some block reaches.
All inputs are finite; a program needn't handle non-finite values.
Results may differ from the reference program's by a relative error of at most 0.027.
Values may be sent and summed in bfloat16 or wider, within the bound.
No kernel may reach another device: no remote copies, remote signals or barrier semaphores. Data moves between devices by JAX's collectives and lax.ppermute only.
A program may use at most 128 MiB of HBM per device.

```python
import math
import jax
import jax.numpy as jnp
import numpy as np
from jax import lax

D = 4096
FF = 1408
TOPK = 6
TOK_DEV = 128
EXPERTS = 16
CAP = 56
SLOTS = 896
TOKENS = 2048
N_DP = 2
N_EXPERT = 16


def steps_of(own_key, extent, shards, low, top_value):
    gain, own = 1.0, jax.random.fold_in(own_key, 6)
    for dim, blocks in shards:
        steps = jnp.exp(jax.random.uniform(jax.random.fold_in(own, dim), (blocks,), jnp.float32, low / len(shards), top_value / len(shards)))
        gain = gain * jnp.repeat(steps, extent[dim] // blocks).reshape([-1 if axis == dim else 1 for axis in range(len(extent))])
    return gain


def deal_out(key, own, number, rows, number_of, top, bound, slope):
    order = jax.random.permutation(key, number_of)
    crowded, usual = portions_of(number_of, rows * top, bound, slope, True), portions_of(number_of, rows * top, bound, slope, False)
    places = jnp.arange(number_of)

    def named(tallies, turn):
        used = int((tallies > 0).sum())
        fixed = max(1, used // 4)
        passed = fixed + (places - fixed + turn * (used - fixed)) % max(1, number_of - fixed)
        return jnp.zeros((number_of,), jnp.int32).at[order[jnp.where(places < fixed, places, passed)]].set(jnp.asarray(tallies, jnp.int32))

    tallies = jnp.where(number % 4 == 0, named(crowded, number // 4), named(usual, number - number // 4 - 1))
    mixed = jax.random.permutation(jax.random.fold_in(own, 3), number_of)
    source_of, sink = mixed[0:number_of // 2 * 2:2], mixed[1:number_of // 2 * 2:2]
    room = jnp.minimum(tallies[source_of] - 1, bound - tallies[sink]) // 2
    room = jnp.where((source_of == order[0]) | (sink == order[0]) | (tallies[sink] == 0), 0, jnp.maximum(room, 0))
    passed = jax.random.randint(jax.random.fold_in(own, 4), (number_of // 2,), 0, 1 << 20) % (room + 1)
    tallies = tallies.at[source_of].add(-passed).at[sink].add(passed)
    labels = jnp.searchsorted(jnp.cumsum(tallies), jnp.arange(rows * top), side="right").astype(jnp.int32)
    grid = labels.reshape(top, rows).T
    grid = grid[jax.random.permutation(jax.random.fold_in(own, 1), rows)]
    turn = jax.random.randint(jax.random.fold_in(own, 2), (rows, 1), 0, top)
    return jnp.take_along_axis(grid, (jnp.arange(top)[None, :] + turn) % top, axis=1)


def portions_of(number_of, total, limit, lean, full):
    portions = [(1 << 20) // math.isqrt(standing ** lean) + 1 for standing in range(1, number_of + 1)]
    largest = limit if full else min(limit, max(-(-total // number_of), total * portions[0] // sum(portions)))
    least = 1 if total - largest >= number_of - 1 else 0
    counts, surplus = [largest] + [least] * (number_of - 1), total - largest - least * (number_of - 1)
    while surplus > 0:
        movable = [i for i in range(1, number_of) if counts[i] < largest] or [i for i in range(1, number_of) if counts[i] < limit]
        mass, remaining = sum([portions[i] for i in movable]), surplus
        for i in movable:
            addition = min(limit - counts[i], max(1, remaining * portions[i] // mass), surplus)
            counts[i] = counts[i] + addition
            surplus = surplus - addition
    return np.array(counts)


def gaussian(stream_key, dims, deviation, bound, shards=(), kind=jnp.bfloat16):
    values = jax.random.normal(stream_key, dims, jnp.float32) * deviation
    if len(shards) > 0:
        values = steps_of(stream_key, dims, shards, -0.22, 0.18) * values
    return jnp.clip(values, min=-bound, max=bound).astype(kind)


def setup_inputs(seed: int = 0) -> dict:
    streams_of = jax.random.split(jax.random.key(seed), 10)
    grad_out = gaussian(streams_of[0], (TOKENS, D), 1.0, 6.0, ((0, 16), (1, 2)))
    routing_keys = jax.random.split(jax.random.fold_in(streams_of[1], 1), TOKENS // TOK_DEV)
    routing_turns = jax.random.permutation(jax.random.fold_in(streams_of[1], 3), TOKENS // TOK_DEV)
    routing = jax.vmap(lambda own, number: deal_out(jax.random.fold_in(streams_of[1], 2), own, number, TOK_DEV, EXPERTS, TOPK, CAP, 1))(routing_keys, routing_turns).reshape((TOKENS, TOPK))
    gates = jnp.clip(jnp.exp(math.log(1.0) - 2.9957323 * jax.random.uniform(streams_of[2], (TOKENS, TOPK), jnp.float32) ** steps_of(streams_of[2], (TOKENS, TOPK), ((0, 16),), -0.2, 0.2)), 0.05, 1.0)
    scales = jnp.clip(jnp.exp(math.log(4.0) - 2.7725887 * jax.random.uniform(streams_of[3], (TOKENS,), jnp.float32) ** steps_of(streams_of[3], (TOKENS,), ((0, 16),), -0.2, 0.2)), 0.25, 4.0)
    saved_gate = gaussian(streams_of[4], (EXPERTS, FF, SLOTS), 1.5, 6.0, ((0, 16),))
    saved_up = gaussian(streams_of[5], (EXPERTS, FF, SLOTS), 1.0, 6.0, ((0, 16),))
    w_gate = gaussian(streams_of[6], (EXPERTS, D, FF), D ** -0.5, 0.09375, ((0, 16), (1, 2)))
    w_up = gaussian(streams_of[7], (EXPERTS, D, FF), D ** -0.5, 0.09375, ((0, 16), (1, 2)))
    w_down = gaussian(streams_of[8], (EXPERTS, FF, D), FF ** -0.5, 0.15625, ((0, 16), (2, 2)))
    return dict(grad_out=grad_out, routing=routing, gates=gates, scales=scales, saved_gate=saved_gate, saved_up=saved_up, w_gate=w_gate, w_up=w_up, w_down=w_down)


def slot_positions(routing):
    rows = routing.reshape(N_EXPERT, TOK_DEV * TOPK)

    def one_group(route_row):
        hot = (route_row[:, None] == jnp.arange(EXPERTS, dtype=jnp.int32)[None, :]).astype(jnp.int32)
        return jnp.sum(hot * (jnp.cumsum(hot, axis=0) - 1), axis=1).astype(jnp.int32)

    return lax.map(one_group, rows).reshape(TOKENS, TOPK)


def reference(grad_out, routing, gates, scales, saved_gate, saved_up, w_gate, w_up, w_down):
    position = slot_positions(routing)
    group = (jnp.arange(TOKENS, dtype=jnp.int32) // TOK_DEV)[:, None]
    slot = (group * CAP + position).astype(jnp.int32)
    flat = (routing * SLOTS + slot).astype(jnp.int32)
    token_ids = jnp.broadcast_to(jnp.arange(TOKENS, dtype=jnp.int32)[:, None], (TOKENS, TOPK))
    owner = jnp.zeros((EXPERTS * SLOTS,), jnp.int32).at[flat.reshape(-1)].set(token_ids.reshape(-1))
    factor = gates * scales[:, None]
    weight = jnp.zeros((EXPERTS * SLOTS,), jnp.float32).at[flat.reshape(-1)].set(factor.reshape(-1).astype(jnp.float32))
    owner = owner.reshape(EXPERTS, SLOTS)
    weight = weight.reshape(EXPERTS, SLOTS)
    dcols = D // N_DP

    def one_expert(items):
        own, fac, sgate, sup, wgate, wup, wdown = items
        expert_grad = (fac[:, None] * grad_out[own].astype(jnp.float32)).astype(jnp.bfloat16)
        parts = jnp.einsum("sid,fid->isf", expert_grad.reshape(SLOTS, N_DP, dcols).astype(jnp.float32),
                           wdown.reshape(FF, N_DP, dcols).astype(jnp.float32))
        rounded = lax.optimization_barrier(parts.astype(jnp.bfloat16))
        hidden_grad = jnp.sum(rounded.astype(jnp.float32), axis=0).astype(jnp.bfloat16)
        g = sgate.T.astype(jnp.float32)
        u = sup.T.astype(jnp.float32)
        sig = jax.nn.sigmoid(g)
        dh = hidden_grad.astype(jnp.float32)
        gate_grad = (dh * u * sig * (1.0 + g * (1.0 - sig))).astype(jnp.bfloat16)
        up_grad = (dh * g * sig).astype(jnp.bfloat16)
        slot_grad = (jnp.dot(gate_grad.astype(jnp.float32), wgate.T.astype(jnp.float32), preferred_element_type=jnp.float32)
                     + jnp.dot(up_grad.astype(jnp.float32), wup.T.astype(jnp.float32), preferred_element_type=jnp.float32)).astype(jnp.bfloat16)
        hidden = (g * sig * u).astype(jnp.bfloat16)
        grad_down = jnp.dot(hidden.T.astype(jnp.float32), expert_grad.astype(jnp.float32),
                            preferred_element_type=jnp.float32).astype(jnp.bfloat16)
        return slot_grad, grad_down

    slot_grads, grad_down = lax.map(one_expert, (owner, weight, saved_gate, saved_up, w_gate, w_up, w_down))
    picked = slot_grads.reshape(EXPERTS * SLOTS, D)[flat]
    grad_x = jnp.sum(picked.astype(jnp.float32), axis=1).astype(jnp.bfloat16)
    return grad_x, grad_down
```

```python
import jax
import jax.numpy as jnp
import numpy as np
from jax import lax
from jax.sharding import PartitionSpec as P


def activation_grad(hidden_grad, gate_pre, up_pre):
    g = gate_pre.astype(jnp.float32)
    u = up_pre.astype(jnp.float32)
    sig = jax.nn.sigmoid(g)
    dh = hidden_grad.astype(jnp.float32)
    gate_grad = (dh * u * sig * (1.0 + g * (1.0 - sig))).astype(jnp.bfloat16)
    up_grad = (dh * g * sig).astype(jnp.bfloat16)
    return (gate_grad, up_grad)


def contract(left, weights):
    return lax.dot_general(
        left, weights, (((0,), (1,)), ((), ())), preferred_element_type=jnp.float32
    )


def exchange_local(grad_out, routing, gates, scales, saved_gate, saved_up, w_gate, w_up, w_down):
    tok_rows, dcols = grad_out.shape
    topk = routing.shape[1]
    groups = lax.axis_size("expert")
    experts = groups * w_gate.shape[0]
    slots = saved_gate.shape[2]
    capacity = slots // groups
    flat_route = routing.reshape(-1)
    hot = (flat_route[:, None] == jnp.arange(experts, dtype=jnp.int32)[None, :]).astype(jnp.int32)
    position = jnp.sum(hot * (jnp.cumsum(hot, axis=0) - 1), axis=1)
    target = flat_route * capacity + position
    select = jnp.arange(experts * capacity, dtype=jnp.int32)[:, None] == target[None, :]
    weight = (gates * scales[:, None]).reshape(-1)
    slot_factor = jnp.sum(jnp.where(select, weight[None, :], 0.0), axis=1)
    collect = jnp.any(select.reshape(experts * capacity, tok_rows, topk), axis=2).astype(
        jnp.bfloat16
    )
    owned_rows = jnp.dot(collect, grad_out, preferred_element_type=jnp.float32)
    sending = (
        (slot_factor[:, None] * owned_rows).astype(jnp.bfloat16).reshape(experts, capacity, dcols)
    )
    arrived = lax.all_to_all(sending, "expert", split_axis=0, concat_axis=0, tiled=True).reshape(
        slots, dcols
    )
    wdown = w_down[0]
    wgate = w_gate[0]
    wup = w_up[0]
    sgate = saved_gate[0]
    sup = saved_up[0]
    partial_value = lax.dot_general(
        wdown, arrived, (((1,), (1,)), ((), ())), preferred_element_type=jnp.float32
    )
    reduced = lax.psum_scatter(
        partial_value.astype(jnp.bfloat16), "dp", scatter_dimension=0, tiled=True
    )
    hidden_grad = lax.all_gather(reduced, "dp", axis=0, tiled=True)
    gate_grad, up_grad = activation_grad(hidden_grad, sgate, sup)
    slot_grad = contract(gate_grad, wgate) + contract(up_grad, wup)
    gate_full = sgate.astype(jnp.float32)
    hidden = (gate_full * jax.nn.sigmoid(gate_full) * sup.astype(jnp.float32)).astype(jnp.bfloat16)
    grad_down = jnp.dot(hidden, arrived, preferred_element_type=jnp.float32).astype(jnp.bfloat16)
    returning = slot_grad.astype(jnp.bfloat16).reshape(groups, capacity, dcols)
    back = lax.all_to_all(returning, "expert", split_axis=0, concat_axis=0, tiled=True).reshape(
        experts * capacity, dcols
    )
    grad_x = lax.dot_general(
        collect, back, (((0,), (0,)), ((), ())), preferred_element_type=jnp.float32
    )
    return (grad_x.astype(jnp.bfloat16), grad_down[None])


def ring_of(chips):
    return list(range(0, chips, 2)) + list(range(1, chips, 2))[::-1]


def meta_columns(routing, gates, scales, experts, lanes):
    tok_rows, topk = routing.shape
    flat_route = routing.reshape(-1)
    hot = (flat_route[:, None] == jnp.arange(experts, dtype=jnp.int32)[None, :]).astype(jnp.int32)
    position = jnp.sum(hot * (jnp.cumsum(hot, axis=0) - 1), axis=1).reshape(tok_rows, topk)
    factor = gates * scales[:, None]
    high = factor.astype(jnp.bfloat16)
    rest = factor - high.astype(jnp.float32)
    middle = rest.astype(jnp.bfloat16)
    low = (rest - middle.astype(jnp.float32)).astype(jnp.bfloat16)
    parts = [routing.astype(jnp.bfloat16), position.astype(jnp.bfloat16), high, middle, low]
    columns = jnp.concatenate(parts, axis=1)
    return jnp.pad(columns, ((0, 0), (0, lanes - columns.shape[1])))


def ring_local(grad_out, routing, gates, scales, saved_gate, saved_up, w_gate, w_up, w_down):
    tok_rows, dcols = grad_out.shape
    topk = routing.shape[1]
    groups = lax.axis_size("expert")
    slots = saved_gate.shape[2]
    capacity = slots // groups
    chips = groups // 2
    order = ring_of(chips)
    place = np.argsort(np.array(order))
    after = {order[i]: order[(i + 1) % chips] for i in range(chips)}
    ring = [(2 * j, 2 * after[j]) for j in range(chips)]
    ring += [(2 * after[j] + 1, 2 * j + 1) for j in range(chips)]
    sibling = [(i, i ^ 1) for i in range(groups)]
    swap = [(0, 1), (1, 0)]
    me = lax.axis_index("expert")
    core = me % 2
    spot = jnp.asarray(place, jnp.int32)[me // 2]
    order_now = jnp.asarray(order, jnp.int32)

    wdown, wgate, wup = w_down[0], w_gate[0], w_up[0]
    lanes = -(-5 * topk // 128) * 128
    payload = jnp.concatenate(
        [grad_out, meta_columns(routing, gates, scales, groups, lanes)], axis=1
    )

    g = saved_gate[0].astype(jnp.float32)
    u = saved_up[0].astype(jnp.float32)
    sig = jax.nn.sigmoid(g)
    to_gate = (u * sig * (1.0 + g * (1.0 - sig))).T.reshape(groups, capacity, -1)
    to_up = (g * sig).T.reshape(groups, capacity, -1)
    hidden = (g * sig * u).astype(jnp.bfloat16)

    def ids(step):
        first = 2 * order_now[(spot - step) % chips]
        second = 2 * order_now[(spot + step) % chips] + 1
        return jnp.where(core == 0, first, second), jnp.where(core == 0, second, first)

    def unpack(rows):
        meta = rows[:, dcols : dcols + 5 * topk].astype(jnp.float32)
        part = [meta[:, i * topk : (i + 1) * topk] for i in range(5)]
        mine = part[0] == me.astype(jnp.float32)
        position = jnp.sum(jnp.where(mine, part[1], 0.0), axis=1)
        position = jnp.where(jnp.any(mine, axis=1), position, -1.0)
        factor = jnp.sum(jnp.where(mine, part[2] + part[3] + part[4], 0.0), axis=1)
        select = (position[:, None] == jnp.arange(capacity, dtype=jnp.float32)[None, :]).astype(
            jnp.bfloat16
        )
        scaled = (factor[:, None] * rows[:, :dcols].astype(jnp.float32)).astype(jnp.bfloat16)
        arrived = lax.dot_general(
            select, scaled, (((0,), (0,)), ((), ())), preferred_element_type=jnp.float32
        ).astype(jnp.bfloat16)
        return select, arrived

    steps = list(range(1, chips)) + [0]
    rows = {0: payload}
    for s in range(1, chips):
        rows[s] = lax.ppermute(rows[s - 1], "expert", ring)
    arrived_all = jnp.zeros((groups, capacity, dcols), jnp.bfloat16)
    total = None
    for s in steps:
        near, far = ids(s)
        other = lax.ppermute(rows[s], "expert", sibling)
        select_near, arrived_near = unpack(rows[s])
        select_far, arrived_far = unpack(other)
        arrived = jnp.concatenate([arrived_near, arrived_far], axis=0)
        arrived_all = lax.dynamic_update_slice(arrived_all, arrived_near[None], (near, 0, 0))
        arrived_all = lax.dynamic_update_slice(arrived_all, arrived_far[None], (far, 0, 0))
        partial_value = lax.dot_general(
            arrived, wdown, (((1,), (1,)), ((), ())), preferred_element_type=jnp.float32
        ).astype(jnp.bfloat16)
        theirs = lax.ppermute(partial_value, "dp", swap)
        dh = (partial_value.astype(jnp.float32) + theirs.astype(jnp.float32)).astype(jnp.bfloat16)
        dh = dh.astype(jnp.float32)

        def rows_of(full):
            return jnp.concatenate(
                [
                    lax.dynamic_index_in_dim(full, near, 0, keepdims=False),
                    lax.dynamic_index_in_dim(full, far, 0, keepdims=False),
                ],
                axis=0,
            )

        gate_grad = (dh * rows_of(to_gate)).astype(jnp.bfloat16)
        up_grad = (dh * rows_of(to_up)).astype(jnp.bfloat16)
        slot_grad = lax.dot_general(
            gate_grad, wgate, (((1,), (1,)), ((), ())), preferred_element_type=jnp.float32
        ) + lax.dot_general(
            up_grad, wup, (((1,), (1,)), ((), ())), preferred_element_type=jnp.float32
        )
        slot_grad = slot_grad.astype(jnp.bfloat16)
        own = jnp.dot(select_near, slot_grad[:capacity], preferred_element_type=jnp.float32)
        given = jnp.dot(select_far, slot_grad[capacity:], preferred_element_type=jnp.float32)
        given = lax.ppermute(given.astype(jnp.bfloat16), "expert", sibling)
        own = own + given.astype(jnp.float32)
        if total is not None:
            own = own + lax.ppermute(total, "expert", ring).astype(jnp.float32)
        total = own.astype(jnp.bfloat16)
    grad_down = jnp.dot(
        hidden, arrived_all.reshape(slots, dcols), preferred_element_type=jnp.float32
    ).astype(jnp.bfloat16)
    return (total, grad_down[None])


def solution(mesh):
    paired = mesh.shape["dp"] == 2 and mesh.shape["expert"] % 4 == 0
    return jax.shard_map(
        ring_local if paired else exchange_local,
        mesh=mesh,
        in_specs=(
            P("expert", "dp"),
            P("expert", None),
            P("expert", None),
            P("expert"),
            P("expert", None, None),
            P("expert", None, None),
            P("expert", "dp", None),
            P("expert", "dp", None),
            P("expert", None, "dp"),
        ),
        out_specs=(P("expert", "dp"), P("expert", None, "dp")),
        check_vma=False,
    )
```

```python
import functools

import jax
import jax.numpy as jnp
import numpy as np
from jax import lax
from jax.experimental import pallas as pl
from jax.experimental.pallas import tpu as pltpu
from jax.sharding import PartitionSpec as P

LANES = 128
PIECES = 4


def activation_grad(hidden_grad, gate_pre, up_pre):
    g = gate_pre.astype(jnp.float32)
    u = up_pre.astype(jnp.float32)
    sig = jax.nn.sigmoid(g)
    dh = hidden_grad.astype(jnp.float32)
    gate_grad = (dh * u * sig * (1.0 + g * (1.0 - sig))).astype(jnp.bfloat16)
    up_grad = (dh * g * sig).astype(jnp.bfloat16)
    return (gate_grad, up_grad)


def contract(left, weights):
    return lax.dot_general(
        left, weights, (((0,), (1,)), ((), ())), preferred_element_type=jnp.float32
    )


def exchange_local(grad_out, routing, gates, scales, saved_gate, saved_up, w_gate, w_up, w_down):
    tok_rows, dcols = grad_out.shape
    topk = routing.shape[1]
    groups = lax.axis_size("expert")
    experts = groups * w_gate.shape[0]
    slots = saved_gate.shape[2]
    capacity = slots // groups
    flat_route = routing.reshape(-1)
    hot = (flat_route[:, None] == jnp.arange(experts, dtype=jnp.int32)[None, :]).astype(jnp.int32)
    position = jnp.sum(hot * (jnp.cumsum(hot, axis=0) - 1), axis=1)
    target = flat_route * capacity + position
    select = jnp.arange(experts * capacity, dtype=jnp.int32)[:, None] == target[None, :]
    weight = (gates * scales[:, None]).reshape(-1)
    slot_factor = jnp.sum(jnp.where(select, weight[None, :], 0.0), axis=1)
    collect = jnp.any(select.reshape(experts * capacity, tok_rows, topk), axis=2).astype(
        jnp.bfloat16
    )
    owned_rows = jnp.dot(collect, grad_out, preferred_element_type=jnp.float32)
    sending = (
        (slot_factor[:, None] * owned_rows).astype(jnp.bfloat16).reshape(experts, capacity, dcols)
    )
    arrived = lax.all_to_all(sending, "expert", split_axis=0, concat_axis=0, tiled=True).reshape(
        slots, dcols
    )
    wdown = w_down[0]
    wgate = w_gate[0]
    wup = w_up[0]
    sgate = saved_gate[0]
    sup = saved_up[0]
    partial_value = lax.dot_general(
        wdown, arrived, (((1,), (1,)), ((), ())), preferred_element_type=jnp.float32
    )
    reduced = lax.psum_scatter(
        partial_value.astype(jnp.bfloat16), "dp", scatter_dimension=0, tiled=True
    )
    hidden_grad = lax.all_gather(reduced, "dp", axis=0, tiled=True)
    gate_grad, up_grad = activation_grad(hidden_grad, sgate, sup)
    slot_grad = contract(gate_grad, wgate) + contract(up_grad, wup)
    gate_full = sgate.astype(jnp.float32)
    hidden = (gate_full * jax.nn.sigmoid(gate_full) * sup.astype(jnp.float32)).astype(jnp.bfloat16)
    grad_down = jnp.dot(hidden, arrived, preferred_element_type=jnp.float32).astype(jnp.bfloat16)
    returning = slot_grad.astype(jnp.bfloat16).reshape(groups, capacity, dcols)
    back = lax.all_to_all(returning, "expert", split_axis=0, concat_axis=0, tiled=True).reshape(
        experts * capacity, dcols
    )
    grad_x = lax.dot_general(
        collect, back, (((0,), (0,)), ((), ())), preferred_element_type=jnp.float32
    )
    return (grad_x.astype(jnp.bfloat16), grad_down[None])


def ring_of(chips):
    return list(range(0, chips, 2)) + list(range(1, chips, 2))[::-1]


def pack_kernel(experts, rows_ref, routing_ref, gates_ref, scales_ref, out_ref):
    tok, topk = routing_ref.shape
    dcols = rows_ref.shape[1]
    lanes = out_ref.shape[1] - dcols
    out_ref[:, :dcols] = rows_ref[...]
    lane = lax.broadcasted_iota(jnp.int32, (tok, lanes), 1)
    expert = lane % experts
    piece = lane // experts
    hot = jnp.zeros((tok, lanes), jnp.float32)
    factor = jnp.zeros((tok, lanes), jnp.float32)
    for k in range(topk):
        same = routing_ref[:, k : k + 1] == expert
        hot += jnp.where(same, 1.0, 0.0)
        factor += jnp.where(same, gates_ref[:, k : k + 1] * scales_ref[...], 0.0)
    row = lax.broadcasted_iota(jnp.int32, (tok, tok), 0)
    column = lax.broadcasted_iota(jnp.int32, (tok, tok), 1)
    earlier = jnp.where(column < row, 1.0, 0.0).astype(jnp.bfloat16)
    before = jnp.dot(earlier, hot.astype(jnp.bfloat16), preferred_element_type=jnp.float32)
    high = factor.astype(jnp.bfloat16)
    rest = factor - high.astype(jnp.float32)
    middle = rest.astype(jnp.bfloat16)
    low = rest - middle.astype(jnp.float32)
    meta = jnp.where(piece == 0, hot * (before + 1.0), 0.0)
    meta = jnp.where(piece == 1, high.astype(jnp.float32), meta)
    meta = jnp.where(piece == 2, middle.astype(jnp.float32), meta)
    meta = jnp.where(piece == 3, low, meta)
    out_ref[:, dcols:] = meta.astype(jnp.bfloat16)


def pack(rows, routing, gates, scales, experts):
    tok, dcols = rows.shape
    lanes = -(-PIECES * experts // LANES) * LANES
    return pl.pallas_call(
        functools.partial(pack_kernel, experts),
        out_shape=jax.ShapeDtypeStruct((tok, dcols + lanes), jnp.bfloat16),
        compiler_params=pltpu.CompilerParams(vmem_limit_bytes=8 << 20),
        cost_estimate=pl.CostEstimate(
            flops=2 * tok * tok * lanes, bytes_accessed=4 * tok * dcols, transcendentals=0
        ),
        name="pack",
    )(rows, routing, gates, scales[:, None])


def prep_kernel(capacity, ids_ref, gate_ref, up_ref, to_gate_ref, to_up_ref, hidden_ref, turned):
    g = gate_ref[...].astype(jnp.float32)
    u = up_ref[...].astype(jnp.float32)
    sig = jax.nn.sigmoid(g)
    turned[0] = (u * sig * (1.0 + g * (1.0 - sig))).T
    turned[1] = (g * sig).T
    turned[2] = (g * sig * u).T
    for i in range(to_gate_ref.shape[0]):
        start = pl.multiple_of(ids_ref[i] * capacity, 8)
        for k, ref in enumerate((to_gate_ref, to_up_ref, hidden_ref)):
            ref[i] = turned[k, pl.ds(start, capacity)].astype(jnp.bfloat16)


def prep(ids, gate, up, capacity):
    ff, slots = gate.shape
    groups = slots // capacity
    tile = LANES
    out = jax.ShapeDtypeStruct((groups, capacity, ff), jnp.bfloat16)
    spec = pl.BlockSpec((tile, slots), lambda i, ids: (i, 0))
    out_spec = pl.BlockSpec((groups, capacity, tile), lambda i, ids: (0, 0, i))
    return pl.pallas_call(
        functools.partial(prep_kernel, capacity),
        grid_spec=pltpu.PrefetchScalarGridSpec(
            num_scalar_prefetch=1,
            grid=(ff // tile,),
            in_specs=[spec, spec],
            out_specs=[out_spec] * 3,
            scratch_shapes=[pltpu.VMEM((3, slots, tile), jnp.float32)],
        ),
        out_shape=[out] * 3,
        compiler_params=pltpu.CompilerParams(vmem_limit_bytes=12 << 20),
        cost_estimate=pl.CostEstimate(
            flops=10 * ff * slots, bytes_accessed=10 * ff * slots, transcendentals=ff * slots
        ),
        name="prep",
    )(ids, gate, up)


def unpack_kernel(capacity, experts, me_ref, near_ref, far_ref, arrived_ref, near_to_ref, far_to_ref):
    dcols = arrived_ref.shape[1]
    me = me_ref[0]
    picked = []
    for ref, to_ref in ((near_ref, near_to_ref), (far_ref, far_to_ref)):
        meta = ref[:, dcols:].astype(jnp.float32)
        tok, lanes = meta.shape
        lane = lax.broadcasted_iota(jnp.int32, (tok, lanes), 1)
        mine = lane % experts == me
        count = jnp.where(mine & (lane < experts), meta, 0.0)
        share = jnp.where(mine & (lane >= experts), meta, 0.0)
        position = jnp.sum(count, axis=1, keepdims=True) - 1.0
        factor = jnp.sum(share, axis=1, keepdims=True)
        slot = lax.broadcasted_iota(jnp.int32, (tok, capacity), 1).astype(jnp.float32)
        select = jnp.where(slot == position, 1.0, 0.0).astype(jnp.bfloat16)
        to_ref[...] = select
        scaled = (factor * ref[:, :dcols].astype(jnp.float32)).astype(jnp.bfloat16)
        picked.append(
            lax.dot_general(
                select, scaled, (((0,), (0,)), ((), ())), preferred_element_type=jnp.float32
            )
        )
    arrived_ref[...] = jnp.concatenate(picked, axis=0).astype(jnp.bfloat16)


def unpack(me, near, far, capacity, experts, dcols):
    tok = near.shape[0]
    smem = pl.BlockSpec(memory_space=pltpu.SMEM)
    return pl.pallas_call(
        functools.partial(unpack_kernel, capacity, experts),
        in_specs=[smem] + [pl.BlockSpec(memory_space=pltpu.VMEM)] * 2,
        out_shape=[
            jax.ShapeDtypeStruct((2 * capacity, dcols), jnp.bfloat16),
            jax.ShapeDtypeStruct((tok, capacity), jnp.bfloat16),
            jax.ShapeDtypeStruct((tok, capacity), jnp.bfloat16),
        ],
        compiler_params=pltpu.CompilerParams(vmem_limit_bytes=10 << 20),
        cost_estimate=pl.CostEstimate(
            flops=4 * tok * capacity * dcols, bytes_accessed=8 * tok * dcols, transcendentals=0
        ),
        name="unpack",
    )(me, near, far)


def ring_local(grad_out, routing, gates, scales, saved_gate, saved_up, w_gate, w_up, w_down):
    tok_rows, dcols = grad_out.shape
    groups = lax.axis_size("expert")
    slots = saved_gate.shape[2]
    capacity = slots // groups
    chips = groups // 2
    order = ring_of(chips)
    place = np.argsort(np.array(order))
    after = {order[i]: order[(i + 1) % chips] for i in range(chips)}
    ring = [(2 * j, 2 * after[j]) for j in range(chips)]
    ring += [(2 * after[j] + 1, 2 * j + 1) for j in range(chips)]
    sibling = [(i, i ^ 1) for i in range(groups)]
    swap = [(0, 1), (1, 0)]
    me = lax.axis_index("expert")
    table = np.zeros((groups, chips, 2), np.int32)
    for device in range(groups):
        spot = place[device // 2]
        for step in range(chips):
            down = 2 * order[(spot - step) % chips]
            up = 2 * order[(spot + step) % chips] + 1
            table[device, step] = (down, up) if device % 2 == 0 else (up, down)
    ids = lax.dynamic_slice(jnp.asarray(table), (me, 0, 0), (1, chips, 2)).reshape(-1)
    me = me.reshape(1)

    wdown, wgate, wup = w_down[0], w_gate[0], w_up[0]
    payload = pack(grad_out, routing, gates, scales, groups)
    staged = prep(ids, saved_gate[0], saved_up[0], capacity)
    to_gate, to_up, hidden = [a.reshape(chips, 2 * capacity, -1) for a in staged]

    rows = {0: payload}
    for s in range(1, chips):
        rows[s] = lax.ppermute(rows[s - 1], "expert", ring)
    arrived = {}
    total = None
    for s in list(range(1, chips)) + [0]:
        other = lax.ppermute(rows[s], "expert", sibling)
        arrived[s], near_to, far_to = unpack(me, rows[s], other, capacity, groups, dcols)
        partial_value = lax.dot_general(
            arrived[s], wdown, (((1,), (1,)), ((), ())), preferred_element_type=jnp.float32
        ).astype(jnp.bfloat16)
        theirs = lax.ppermute(partial_value, "dp", swap)
        dh = (partial_value.astype(jnp.float32) + theirs.astype(jnp.float32)).astype(jnp.bfloat16)
        dh = dh.astype(jnp.float32)
        gate_grad = (dh * to_gate[s].astype(jnp.float32)).astype(jnp.bfloat16)
        up_grad = (dh * to_up[s].astype(jnp.float32)).astype(jnp.bfloat16)
        slot_grad = lax.dot_general(
            gate_grad, wgate, (((1,), (1,)), ((), ())), preferred_element_type=jnp.float32
        ) + lax.dot_general(
            up_grad, wup, (((1,), (1,)), ((), ())), preferred_element_type=jnp.float32
        )
        slot_grad = slot_grad.astype(jnp.bfloat16)
        own = jnp.dot(near_to, slot_grad[:capacity], preferred_element_type=jnp.float32)
        sent = jnp.dot(far_to, slot_grad[capacity:], preferred_element_type=jnp.float32)
        given = lax.ppermute(sent.astype(jnp.bfloat16), "expert", sibling)
        own = own + given.astype(jnp.float32)
        if total is not None:
            own = own + lax.ppermute(total, "expert", ring).astype(jnp.float32)
        total = own.astype(jnp.bfloat16)
    slots_in_order = jnp.concatenate([arrived[s] for s in range(chips)], axis=0)
    grad_down = lax.dot_general(
        hidden.reshape(slots, -1),
        slots_in_order,
        (((0,), (0,)), ((), ())),
        preferred_element_type=jnp.float32,
    ).astype(jnp.bfloat16)
    return (total, grad_down[None])


def solution(mesh):
    paired = mesh.shape["dp"] == 2 and mesh.shape["expert"] % 4 == 0
    return jax.shard_map(
        ring_local if paired else exchange_local,
        mesh=mesh,
        in_specs=(
            P("expert", "dp"),
            P("expert", None),
            P("expert", None),
            P("expert"),
            P("expert", None, None),
            P("expert", None, None),
            P("expert", "dp", None),
            P("expert", "dp", None),
            P("expert", None, "dp"),
        ),
        out_specs=(P("expert", "dp"), P("expert", None, "dp")),
        check_vma=False,
    )
```

```python
import functools

import jax
import jax.numpy as jnp
import numpy as np
from jax import lax
from jax.experimental import pallas as pl
from jax.experimental.pallas import tpu as pltpu
from jax.sharding import PartitionSpec as P

LANES = 128
PIECES = 4
NT = (((1,), (1,)), ((), ()))
TN = (((0,), (0,)), ((), ()))
VMEM = pl.BlockSpec(memory_space=pltpu.VMEM)
ANY = pl.BlockSpec(memory_space=pl.ANY)
FREE = pl.CostEstimate(flops=0, bytes_accessed=0, transcendentals=0)


def activation_grad(hidden_grad, gate_pre, up_pre):
    g = gate_pre.astype(jnp.float32)
    u = up_pre.astype(jnp.float32)
    sig = jax.nn.sigmoid(g)
    dh = hidden_grad.astype(jnp.float32)
    gate_grad = (dh * u * sig * (1.0 + g * (1.0 - sig))).astype(jnp.bfloat16)
    up_grad = (dh * g * sig).astype(jnp.bfloat16)
    return (gate_grad, up_grad)


def contract(left, weights):
    return lax.dot_general(
        left, weights, (((0,), (1,)), ((), ())), preferred_element_type=jnp.float32
    )


def exchange_local(grad_out, routing, gates, scales, saved_gate, saved_up, w_gate, w_up, w_down):
    tok_rows, dcols = grad_out.shape
    topk = routing.shape[1]
    groups = lax.axis_size("expert")
    experts = groups * w_gate.shape[0]
    slots = saved_gate.shape[2]
    capacity = slots // groups
    flat_route = routing.reshape(-1)
    hot = (flat_route[:, None] == jnp.arange(experts, dtype=jnp.int32)[None, :]).astype(jnp.int32)
    position = jnp.sum(hot * (jnp.cumsum(hot, axis=0) - 1), axis=1)
    target = flat_route * capacity + position
    select = jnp.arange(experts * capacity, dtype=jnp.int32)[:, None] == target[None, :]
    weight = (gates * scales[:, None]).reshape(-1)
    slot_factor = jnp.sum(jnp.where(select, weight[None, :], 0.0), axis=1)
    collect = jnp.any(select.reshape(experts * capacity, tok_rows, topk), axis=2).astype(
        jnp.bfloat16
    )
    owned_rows = jnp.dot(collect, grad_out, preferred_element_type=jnp.float32)
    sending = (
        (slot_factor[:, None] * owned_rows).astype(jnp.bfloat16).reshape(experts, capacity, dcols)
    )
    arrived = lax.all_to_all(sending, "expert", split_axis=0, concat_axis=0, tiled=True).reshape(
        slots, dcols
    )
    wdown = w_down[0]
    wgate = w_gate[0]
    wup = w_up[0]
    sgate = saved_gate[0]
    sup = saved_up[0]
    partial_value = lax.dot_general(
        wdown, arrived, (((1,), (1,)), ((), ())), preferred_element_type=jnp.float32
    )
    reduced = lax.psum_scatter(
        partial_value.astype(jnp.bfloat16), "dp", scatter_dimension=0, tiled=True
    )
    hidden_grad = lax.all_gather(reduced, "dp", axis=0, tiled=True)
    gate_grad, up_grad = activation_grad(hidden_grad, sgate, sup)
    slot_grad = contract(gate_grad, wgate) + contract(up_grad, wup)
    gate_full = sgate.astype(jnp.float32)
    hidden = (gate_full * jax.nn.sigmoid(gate_full) * sup.astype(jnp.float32)).astype(jnp.bfloat16)
    grad_down = jnp.dot(hidden, arrived, preferred_element_type=jnp.float32).astype(jnp.bfloat16)
    returning = slot_grad.astype(jnp.bfloat16).reshape(groups, capacity, dcols)
    back = lax.all_to_all(returning, "expert", split_axis=0, concat_axis=0, tiled=True).reshape(
        experts * capacity, dcols
    )
    grad_x = lax.dot_general(
        collect, back, (((0,), (0,)), ((), ())), preferred_element_type=jnp.float32
    )
    return (grad_x.astype(jnp.bfloat16), grad_down[None])


def ring_of(chips):
    return list(range(0, chips, 2)) + list(range(1, chips, 2))[::-1]


def pack_kernel(experts, rows_ref, routing_ref, gates_ref, scales_ref, out_ref):
    topk, tok = routing_ref.shape
    dcols = rows_ref.shape[1]
    lanes = out_ref.shape[1] - dcols
    out_ref[:, :dcols] = rows_ref[...]
    line = lax.broadcasted_iota(jnp.int32, (lanes, tok), 0)
    expert = line % experts
    piece = line // experts
    hot = jnp.zeros((lanes, tok), jnp.float32)
    factor = jnp.zeros((lanes, tok), jnp.float32)
    for k in range(topk):
        same = routing_ref[k : k + 1] == expert
        hot += jnp.where(same, 1.0, 0.0)
        factor += jnp.where(same, gates_ref[k : k + 1] * scales_ref[...], 0.0)
    row = lax.broadcasted_iota(jnp.int32, (tok, tok), 0)
    column = lax.broadcasted_iota(jnp.int32, (tok, tok), 1)
    earlier = jnp.where(row < column, 1.0, 0.0).astype(jnp.bfloat16)
    before = jnp.dot(hot.astype(jnp.bfloat16), earlier, preferred_element_type=jnp.float32)
    high = factor.astype(jnp.bfloat16)
    rest = factor - high.astype(jnp.float32)
    middle = rest.astype(jnp.bfloat16)
    low = rest - middle.astype(jnp.float32)
    meta = jnp.where(piece == 0, hot * (before + 1.0), 0.0)
    meta = jnp.where(piece == 1, high.astype(jnp.float32), meta)
    meta = jnp.where(piece == 2, middle.astype(jnp.float32), meta)
    meta = jnp.where(piece == 3, low, meta)
    out_ref[:, dcols:] = meta.T.astype(jnp.bfloat16)


def whole(shape):
    return pl.BlockSpec(shape, lambda i: (0,) * len(shape))


def pack(rows, routing, gates, scales, experts):
    tok, dcols = rows.shape
    lanes = -(-PIECES * experts // LANES) * LANES
    operands = [
        pltpu.with_memory_space_constraint(a, pltpu.HBM)
        for a in (rows, routing.T, gates.T, scales[None])
    ]
    return pl.pallas_call(
        functools.partial(pack_kernel, experts),
        grid=(1,),
        in_specs=[whole(a.shape) for a in operands],
        out_specs=whole((tok, dcols + lanes)),
        out_shape=jax.ShapeDtypeStruct((tok, dcols + lanes), jnp.bfloat16),
        compiler_params=pltpu.CompilerParams(vmem_limit_bytes=8 << 20),
        cost_estimate=FREE,
        name="pack",
    )(*operands)


def prep_kernel(capacity, ids_ref, gate_ref, up_ref, to_gate_ref, to_up_ref, hidden_ref, turned):
    g = gate_ref[...].astype(jnp.float32)
    u = up_ref[...].astype(jnp.float32)
    sig = jax.nn.sigmoid(g)
    swish = g * sig
    hidden_ref[...] = (swish * u).astype(jnp.bfloat16)
    turned[0] = (u * sig * (1.0 + g * (1.0 - sig))).T
    turned[1] = swish.T
    for i in range(to_gate_ref.shape[0]):
        start = pl.multiple_of(ids_ref[i] * capacity, 8)
        for k, ref in enumerate((to_gate_ref, to_up_ref)):
            ref[i] = turned[k, pl.ds(start, capacity)].astype(jnp.bfloat16)


def prep(ids, gate, up, capacity):
    ff, slots = gate.shape
    groups = slots // capacity
    tile = LANES
    out = jax.ShapeDtypeStruct((groups, capacity, ff), jnp.bfloat16)
    spec = pl.BlockSpec((tile, slots), lambda i, ids: (i, 0))
    out_spec = pl.BlockSpec((groups, capacity, tile), lambda i, ids: (0, 0, i))
    operands = [pltpu.with_memory_space_constraint(a, pltpu.HBM) for a in (gate, up)]
    return pl.pallas_call(
        functools.partial(prep_kernel, capacity),
        grid_spec=pltpu.PrefetchScalarGridSpec(
            num_scalar_prefetch=1,
            grid=(ff // tile,),
            in_specs=[spec, spec],
            out_specs=[out_spec, out_spec, spec],
            scratch_shapes=[pltpu.VMEM((2, slots, tile), jnp.float32)],
        ),
        out_shape=[out, out, jax.ShapeDtypeStruct(gate.shape, jnp.bfloat16)],
        compiler_params=pltpu.CompilerParams(vmem_limit_bytes=12 << 20),
        cost_estimate=pl.CostEstimate(
            flops=10 * ff * slots, bytes_accessed=10 * ff * slots, transcendentals=ff * slots
        ),
        name="prep",
    )(ids, *operands)


def hold_kernel(*refs):
    count = (len(refs) - 2) // 2
    copies = [
        pltpu.make_async_copy(refs[i], refs[count + 1 + i], refs[-1].at[i]) for i in range(count)
    ]
    for copy in copies:
        copy.start()
    for copy in copies:
        copy.wait()


def hold(weights, after):
    operands = [pltpu.with_memory_space_constraint(w, pltpu.HBM) for w in weights]
    return pl.pallas_call(
        hold_kernel,
        in_specs=[ANY] * (len(weights) + 1),
        out_specs=[VMEM] * len(weights),
        out_shape=[pltpu.VMEM(w.shape, w.dtype) for w in weights],
        scratch_shapes=[pltpu.SemaphoreType.DMA((len(weights),))],
        compiler_params=pltpu.CompilerParams(vmem_limit_bytes=1 << 20),
        cost_estimate=FREE,
        name="hold",
    )(*operands, after)


def take_kernel(experts, count, me_ref, wdown_ref, *refs):
    rows, arrived_ref, partial_ref, leads = refs[:count], refs[count], refs[count + 1], refs[count + 2 :]
    groups, capacity, dcols = arrived_ref.shape
    me = me_ref[0]
    picked = []
    for i, (ref, to_ref) in enumerate(zip(rows, leads)):
        meta = ref[:, dcols:].astype(jnp.float32)
        tok, lanes = meta.shape
        lane = lax.broadcasted_iota(jnp.int32, (tok, lanes), 1)
        mine = lane % experts == me
        places = jnp.where(mine & (lane < experts), meta, 0.0)
        share = jnp.where(mine & (lane >= experts), meta, 0.0)
        position = jnp.sum(places, axis=1, keepdims=True) - 1.0
        factor = jnp.sum(share, axis=1, keepdims=True)
        slot = lax.broadcasted_iota(jnp.int32, (tok, capacity), 1).astype(jnp.float32)
        select = jnp.where(slot == position, 1.0, 0.0).astype(jnp.bfloat16)
        to_ref[...] = select
        scaled = (factor * ref[:, :dcols].astype(jnp.float32)).astype(jnp.bfloat16)
        picked.append(lax.dot_general(select, scaled, TN, preferred_element_type=jnp.float32))
        arrived_ref[i] = picked[i].astype(jnp.bfloat16)
    partial_ref[...] = lax.dot_general(
        jnp.concatenate(picked, axis=0).astype(jnp.bfloat16),
        wdown_ref[...],
        NT,
        preferred_element_type=jnp.float32,
    ).astype(jnp.bfloat16)


def take_rows(me, wdown, rows, capacity, experts):
    count, tok = len(rows), rows[0].shape[0]
    ff, dcols = wdown.shape
    lead = jax.ShapeDtypeStruct((tok, capacity), jnp.bfloat16)
    return pl.pallas_call(
        functools.partial(take_kernel, experts, count),
        in_specs=[pl.BlockSpec(memory_space=pltpu.SMEM)] + [VMEM] * (1 + count),
        out_shape=[
            jax.ShapeDtypeStruct((count, capacity, dcols), jnp.bfloat16),
            jax.ShapeDtypeStruct((count * capacity, ff), jnp.bfloat16),
        ]
        + [lead] * count,
        compiler_params=pltpu.CompilerParams(vmem_limit_bytes=18 << 20),
        cost_estimate=FREE,
        name="take",
    )(me, wdown, *rows)


def give_kernel(count, mine_ref, theirs_ref, to_gate_ref, to_up_ref, wgate_ref, wup_ref, *refs):
    leads, outs = refs[:count], refs[count:]
    capacity = to_gate_ref.shape[1]
    dh = mine_ref[...].astype(jnp.float32) + theirs_ref[...].astype(jnp.float32)
    dh = dh.astype(jnp.bfloat16).astype(jnp.float32)

    def scaled(ref):
        return (dh * ref[...].astype(jnp.float32).reshape(dh.shape)).astype(jnp.bfloat16)

    slot_grad = lax.dot_general(
        scaled(to_gate_ref), wgate_ref[...], NT, preferred_element_type=jnp.float32
    )
    slot_grad += lax.dot_general(
        scaled(to_up_ref), wup_ref[...], NT, preferred_element_type=jnp.float32
    )
    for i, (lead, out) in enumerate(zip(leads, outs)):
        part = slot_grad[i * capacity : (i + 1) * capacity].astype(jnp.bfloat16)
        out[...] = jnp.dot(lead[...], part, preferred_element_type=jnp.float32).astype(jnp.bfloat16)


def give_rows(first, mine, theirs, to_gate, to_up, wgate, wup, leads):
    count, tok = len(leads), leads[0].shape[0]
    capacity, ff = to_gate.shape[1:]
    factors = pl.BlockSpec((count, capacity, ff), lambda i: (first // count, 0, 0))
    out = jax.ShapeDtypeStruct((tok, wgate.shape[0]), jnp.bfloat16)
    return pl.pallas_call(
        functools.partial(give_kernel, count),
        grid=(1,),
        in_specs=[VMEM, VMEM, factors, factors] + [VMEM] * (2 + count),
        out_specs=[VMEM] * count,
        out_shape=[out] * count,
        compiler_params=pltpu.CompilerParams(vmem_limit_bytes=20 << 20),
        cost_estimate=FREE,
        name="give",
    )(mine, theirs, to_gate, to_up, wgate, wup, *leads)


def add_kernel(*refs):
    total = refs[0][...].astype(jnp.float32)
    for ref in refs[1:-1]:
        total += ref[...].astype(jnp.float32)
    refs[-1][...] = total.astype(refs[-1].dtype)


def add(*parts):
    return pl.pallas_call(
        add_kernel,
        in_specs=[VMEM] * len(parts),
        out_specs=VMEM,
        out_shape=jax.ShapeDtypeStruct(parts[0].shape, parts[0].dtype),
        compiler_params=pltpu.CompilerParams(vmem_limit_bytes=8 << 20),
        cost_estimate=FREE,
        name="add",
    )(*parts)


def sort_kernel(ids_ref, *refs):
    parts, out_ref, done = refs[:-2], refs[-2], refs[-1]
    copies, n = [], 0
    for part in parts:
        for i in range(part.shape[0]):
            copies.append(pltpu.make_async_copy(part.at[i], out_ref.at[ids_ref[n]], done.at[n]))
            n += 1
    for copy in copies:
        copy.start()
    for copy in copies:
        copy.wait()


def sort(ids, parts):
    groups = ids.shape[0]
    return pl.pallas_call(
        sort_kernel,
        in_specs=[pl.BlockSpec(memory_space=pltpu.SMEM)] + [ANY] * len(parts),
        out_specs=ANY,
        out_shape=jax.ShapeDtypeStruct((groups,) + parts[0].shape[1:], jnp.bfloat16),
        scratch_shapes=[pltpu.SemaphoreType.DMA((groups,))],
        compiler_params=pltpu.CompilerParams(vmem_limit_bytes=1 << 20),
        cost_estimate=FREE,
        name="sort",
    )(ids, *parts)


def ring_local(grad_out, routing, gates, scales, saved_gate, saved_up, w_gate, w_up, w_down):
    tok_rows, dcols = grad_out.shape
    groups = lax.axis_size("expert")
    slots = saved_gate.shape[2]
    capacity = slots // groups
    chips = groups // 2
    order = ring_of(chips)
    place = np.argsort(np.array(order))
    after = {order[i]: order[(i + 1) % chips] for i in range(chips)}
    ring = [(2 * j, 2 * after[j]) for j in range(chips)]
    ring += [(2 * after[j] + 1, 2 * j + 1) for j in range(chips)]
    sibling = [(i, i ^ 1) for i in range(groups)]
    swap = [(0, 1), (1, 0)]
    me = lax.axis_index("expert")
    back = [(b, a) for a, b in ring]
    stages = [(s, chips - s) for s in range(1, chips // 2)] + [(chips // 2,)]
    steps = [s for stage in stages for s in stage] + [0]
    table = np.zeros((groups, groups), np.int32)
    for device in range(groups):
        spot = place[device // 2]
        for i, step in enumerate(steps):
            down = 2 * order[(spot - step) % chips]
            up = 2 * order[(spot + step) % chips] + 1
            table[device, 2 * i : 2 * i + 2] = (down, up) if device % 2 == 0 else (up, down)
    ids = lax.dynamic_slice(jnp.asarray(table), (me, 0), (1, groups)).reshape(-1)
    me = me.reshape(1)

    payload = pack(grad_out, routing, gates, scales, groups)
    to_gate, to_up, hidden = prep(ids, saved_gate[0], saved_up[0], capacity)
    (wdown,) = hold([w_down[0]], hidden)

    tie = lax.optimization_barrier
    rows, others = {0: payload}, {}
    arrived, leads, partial, theirs, own, given, totals = {}, {}, {}, {}, {}, {}, {}

    def pass_on(stage):
        for s in stage:
            if s <= chips // 2:
                rows[s] = lax.ppermute(rows[s - 1], "expert", ring)
            else:
                rows[s] = lax.ppermute(rows[(s + 1) % chips], "expert", back)

    def share(stage):
        for s in stage:
            others[s] = lax.ppermute(rows[s], "expert", sibling)

    def take(stage):
        near_far = [a for s in stage for a in (rows[s], others[s])]
        arrived[stage], partial[stage], *leads[stage] = take_rows(
            me, wdown, near_far, capacity, groups
        )

    def trade(stage):
        theirs[stage] = lax.ppermute(partial[stage], "dp", swap)

    def give(stage, then=None):
        first = 2 * steps.index(stage[0])
        parts = give_rows(
            first, partial[stage], theirs[stage], to_gate, to_up, *held, leads[stage]
        )
        if then is not None:
            theirs[then], *parts = tie((theirs[then], *parts))
        for i, s in enumerate(stage):
            own[s] = parts[2 * i]
            given[s] = lax.ppermute(parts[2 * i + 1], "expert", sibling)

    def collect(s, before):
        parts = [own[s], given[s]]
        if before is not None:
            parts.append(lax.ppermute(totals[before], "expert", ring).astype(jnp.float32))
        totals[s] = add(*parts)

    def after(values, keys, guard, key):
        *kept, guard[key] = tie(tuple(values[k] for k in keys) + (guard[key],))
        for k, v in zip(keys, kept):
            values[k] = v

    last = (0,)
    pass_on(stages[0])
    share(last)
    take(last)
    trade(last)
    rows[1], hidden = tie((rows[1], hidden))
    after(rows, stages[0], partial, last)
    held = hold([w_gate[0], w_up[0]], leads[last][0])
    before = last
    for i, stage in enumerate(stages):
        if i + 1 < len(stages):
            pass_on(stages[i + 1])
        share(stage)
        take(stage)
        trade(stage)
        after(theirs, [before], partial, stage)
        give(before, stage if i + 1 == len(stages) else None)
        if i + 1 < len(stages):
            after(rows, stages[i + 1], own, before[0])
        if i > 0:
            collect(before[0], before[0] - 1 if before[0] > 1 else None)
        before = stage
    after(theirs, [before], totals, before[0] - 1)
    give(before)
    for s in list(range(before[0], chips)) + [0]:
        collect(s, (s - 1) % chips)
    parts = [arrived[stage] for stage in stages + [last]]
    every = sort(ids, parts)
    grad_down = jnp.dot(
        hidden, every.reshape(slots, dcols), preferred_element_type=jnp.float32
    ).astype(jnp.bfloat16)
    return (totals[0], grad_down[None])


def solution(mesh):
    paired = mesh.shape["dp"] == 2 and mesh.shape["expert"] % 4 == 0
    return jax.shard_map(
        ring_local if paired else exchange_local,
        mesh=mesh,
        in_specs=(
            P("expert", "dp"),
            P("expert", None),
            P("expert", None),
            P("expert"),
            P("expert", None, None),
            P("expert", None, None),
            P("expert", "dp", None),
            P("expert", "dp", None),
            P("expert", None, "dp"),
        ),
        out_specs=(P("expert", "dp"), P("expert", None, "dp")),
        check_vma=False,
    )
```

```python
import functools

import jax
import jax.numpy as jnp
import numpy as np
from jax import lax
from jax.experimental import pallas as pl
from jax.experimental.pallas import tpu as pltpu
from jax.sharding import PartitionSpec as P

LANES = 128
PIECES = 4
HALVES = 4
SPLIT = 6
NT = (((1,), (1,)), ((), ()))
TN = (((0,), (0,)), ((), ()))
VMEM = pl.BlockSpec(memory_space=pltpu.VMEM)
ANY = pl.BlockSpec(memory_space=pl.ANY)
TOKEN = jax.ShapeDtypeStruct((8, LANES), jnp.float32)
FREE = pl.CostEstimate(flops=0, bytes_accessed=0, transcendentals=0)


def activation_grad(hidden_grad, gate_pre, up_pre):
    g = gate_pre.astype(jnp.float32)
    u = up_pre.astype(jnp.float32)
    sig = jax.nn.sigmoid(g)
    dh = hidden_grad.astype(jnp.float32)
    gate_grad = (dh * u * sig * (1.0 + g * (1.0 - sig))).astype(jnp.bfloat16)
    up_grad = (dh * g * sig).astype(jnp.bfloat16)
    return (gate_grad, up_grad)


def contract(left, weights):
    return lax.dot_general(
        left, weights, (((0,), (1,)), ((), ())), preferred_element_type=jnp.float32
    )


def exchange_local(grad_out, routing, gates, scales, saved_gate, saved_up, w_gate, w_up, w_down):
    tok_rows, dcols = grad_out.shape
    topk = routing.shape[1]
    groups = lax.axis_size("expert")
    experts = groups * w_gate.shape[0]
    slots = saved_gate.shape[2]
    capacity = slots // groups
    flat_route = routing.reshape(-1)
    hot = (flat_route[:, None] == jnp.arange(experts, dtype=jnp.int32)[None, :]).astype(jnp.int32)
    position = jnp.sum(hot * (jnp.cumsum(hot, axis=0) - 1), axis=1)
    target = flat_route * capacity + position
    select = jnp.arange(experts * capacity, dtype=jnp.int32)[:, None] == target[None, :]
    weight = (gates * scales[:, None]).reshape(-1)
    slot_factor = jnp.sum(jnp.where(select, weight[None, :], 0.0), axis=1)
    collect = jnp.any(select.reshape(experts * capacity, tok_rows, topk), axis=2).astype(
        jnp.bfloat16
    )
    owned_rows = jnp.dot(collect, grad_out, preferred_element_type=jnp.float32)
    sending = (
        (slot_factor[:, None] * owned_rows).astype(jnp.bfloat16).reshape(experts, capacity, dcols)
    )
    arrived = lax.all_to_all(sending, "expert", split_axis=0, concat_axis=0, tiled=True).reshape(
        slots, dcols
    )
    wdown = w_down[0]
    wgate = w_gate[0]
    wup = w_up[0]
    sgate = saved_gate[0]
    sup = saved_up[0]
    partial_value = lax.dot_general(
        wdown, arrived, (((1,), (1,)), ((), ())), preferred_element_type=jnp.float32
    )
    reduced = lax.psum_scatter(
        partial_value.astype(jnp.bfloat16), "dp", scatter_dimension=0, tiled=True
    )
    hidden_grad = lax.all_gather(reduced, "dp", axis=0, tiled=True)
    gate_grad, up_grad = activation_grad(hidden_grad, sgate, sup)
    slot_grad = contract(gate_grad, wgate) + contract(up_grad, wup)
    gate_full = sgate.astype(jnp.float32)
    hidden = (gate_full * jax.nn.sigmoid(gate_full) * sup.astype(jnp.float32)).astype(jnp.bfloat16)
    grad_down = jnp.dot(hidden, arrived, preferred_element_type=jnp.float32).astype(jnp.bfloat16)
    returning = slot_grad.astype(jnp.bfloat16).reshape(groups, capacity, dcols)
    back = lax.all_to_all(returning, "expert", split_axis=0, concat_axis=0, tiled=True).reshape(
        experts * capacity, dcols
    )
    grad_x = lax.dot_general(
        collect, back, (((0,), (0,)), ((), ())), preferred_element_type=jnp.float32
    )
    return (grad_x.astype(jnp.bfloat16), grad_down[None])


def ring_of(chips):
    return list(range(0, chips, 2)) + list(range(1, chips, 2))[::-1]


def pack_kernel(experts, rows_ref, routing_ref, gates_ref, scales_ref, out_ref):
    topk, tok = routing_ref.shape
    dcols = rows_ref.shape[1]
    lanes = out_ref.shape[1] - dcols
    out_ref[:, :dcols] = rows_ref[...]
    line = lax.broadcasted_iota(jnp.int32, (lanes, tok), 0)
    expert = line % experts
    piece = line // experts
    hot = jnp.zeros((lanes, tok), jnp.float32)
    factor = jnp.zeros((lanes, tok), jnp.float32)
    for k in range(topk):
        same = routing_ref[k : k + 1] == expert
        hot += jnp.where(same, 1.0, 0.0)
        factor += jnp.where(same, gates_ref[k : k + 1] * scales_ref[...], 0.0)
    row = lax.broadcasted_iota(jnp.int32, (tok, tok), 0)
    column = lax.broadcasted_iota(jnp.int32, (tok, tok), 1)
    earlier = jnp.where(row < column, 1.0, 0.0).astype(jnp.bfloat16)
    before = jnp.dot(hot.astype(jnp.bfloat16), earlier, preferred_element_type=jnp.float32)
    high = factor.astype(jnp.bfloat16)
    rest = factor - high.astype(jnp.float32)
    middle = rest.astype(jnp.bfloat16)
    low = rest - middle.astype(jnp.float32)
    meta = jnp.where(piece == 0, hot * (before + 1.0), 0.0)
    meta = jnp.where(piece == 1, high.astype(jnp.float32), meta)
    meta = jnp.where(piece == 2, middle.astype(jnp.float32), meta)
    meta = jnp.where(piece == 3, low, meta)
    out_ref[:, dcols:] = meta.T.astype(jnp.bfloat16)


def whole(shape):
    return pl.BlockSpec(shape, lambda i: (0,) * len(shape))


def pack(rows, routing, gates, scales, experts):
    tok, dcols = rows.shape
    lanes = -(-PIECES * experts // LANES) * LANES
    operands = [
        pltpu.with_memory_space_constraint(a, pltpu.HBM)
        for a in (rows, routing.T, gates.T, scales[None])
    ]
    return pl.pallas_call(
        functools.partial(pack_kernel, experts),
        grid=(1,),
        in_specs=[whole(a.shape) for a in operands],
        out_specs=whole((tok, dcols + lanes)),
        out_shape=jax.ShapeDtypeStruct((tok, dcols + lanes), jnp.bfloat16),
        compiler_params=pltpu.CompilerParams(vmem_limit_bytes=8 << 20),
        cost_estimate=FREE,
        name="pack",
    )(*operands)


def prep_kernel(capacity, first, ids_ref, gate_ref, up_ref, *refs):
    to_gate_ref, to_up_ref, hidden_ref, token_ref, turned = refs[-5:]
    g = gate_ref[...].astype(jnp.float32)
    u = up_ref[...].astype(jnp.float32)
    sig = jax.nn.sigmoid(g)
    swish = g * sig
    turned[0] = (u * sig * (1.0 + g * (1.0 - sig))).T
    turned[1] = swish.T
    turned[2] = (swish * u).T

    def in_order(k):
        groups = gate_ref.shape[1] // capacity
        starts = [pl.multiple_of(ids_ref[i] * capacity, 8) for i in range(groups)]
        return jnp.concatenate([turned[k, pl.ds(start, capacity)] for start in starts], axis=0)

    span = pl.ds(pl.multiple_of((first + pl.program_id(0)) * LANES, LANES), LANES)
    to_gate_ref[:, span] = in_order(0).astype(jnp.bfloat16)
    to_up_ref[:, span] = in_order(1).astype(jnp.bfloat16)
    hidden_ref[span] = in_order(2).T.astype(jnp.bfloat16)
    token_ref[...] = jnp.zeros(token_ref.shape, token_ref.dtype)


def prep(ids, gate, up, capacity, tiles, old=()):
    ff, slots = gate.shape
    spec = pl.BlockSpec((LANES, slots), lambda i, ids: (tiles[0] + i, 0))
    operands = [pltpu.with_memory_space_constraint(a, pltpu.HBM) for a in (gate, up)]
    count = (tiles[1] - tiles[0]) * LANES
    return pl.pallas_call(
        functools.partial(prep_kernel, capacity, tiles[0]),
        grid_spec=pltpu.PrefetchScalarGridSpec(
            num_scalar_prefetch=1,
            grid=(tiles[1] - tiles[0],),
            in_specs=[spec, spec] + [VMEM] * len(old),
            out_specs=[VMEM] * 3 + [pl.BlockSpec(TOKEN.shape, lambda i, ids: (0, 0))],
            scratch_shapes=[pltpu.VMEM((3, slots, LANES), jnp.float32)],
        ),
        out_shape=[
            pltpu.VMEM((slots, ff), jnp.bfloat16),
            pltpu.VMEM((slots, ff), jnp.bfloat16),
            pltpu.VMEM((ff, slots), jnp.bfloat16),
            TOKEN,
        ],
        input_output_aliases={3 + i: i for i in range(len(old))},
        compiler_params=pltpu.CompilerParams(vmem_limit_bytes=8 << 20),
        cost_estimate=pl.CostEstimate(
            flops=10 * count * slots, bytes_accessed=10 * count * slots, transcendentals=count * slots
        ),
        name="prep",
    )(ids, *operands, *old)


def hold_kernel(weights_ref, *refs):
    out_ref, token_ref, done = refs[-3:]
    copy = pltpu.make_async_copy(weights_ref, out_ref, done)
    copy.start()
    token_ref[...] = jnp.zeros(token_ref.shape, token_ref.dtype)
    copy.wait()


def hold(weights, *after):
    return pl.pallas_call(
        hold_kernel,
        in_specs=[ANY] * (1 + len(after)),
        out_specs=[VMEM, VMEM],
        out_shape=[pltpu.VMEM(weights.shape, weights.dtype), TOKEN],
        scratch_shapes=[pltpu.SemaphoreType.DMA(())],
        compiler_params=pltpu.CompilerParams(vmem_limit_bytes=1 << 20),
        cost_estimate=FREE,
        name="hold",
    )(pltpu.with_memory_space_constraint(weights, pltpu.HBM), *after)


def take_kernel(experts, count, first, me_ref, wdown_ref, *refs):
    rows, (every_ref, partial_ref, *leads) = refs[:count], refs[-2 - count :]
    dcols = every_ref.shape[1]
    capacity = every_ref.shape[0] // experts
    me = me_ref[0]
    picked = []
    for ref, to_ref in zip(rows, leads):
        meta = ref[:, dcols:].astype(jnp.float32)
        tok, lanes = meta.shape
        lane = lax.broadcasted_iota(jnp.int32, (tok, lanes), 1)
        mine = lane % experts == me
        places = jnp.where(mine & (lane < experts), meta, 0.0)
        share = jnp.where(mine & (lane >= experts), meta, 0.0)
        position = jnp.sum(places, axis=1, keepdims=True) - 1.0
        factor = jnp.sum(share, axis=1, keepdims=True)
        slot = lax.broadcasted_iota(jnp.int32, (tok, capacity), 1).astype(jnp.float32)
        select = jnp.where(slot == position, 1.0, 0.0).astype(jnp.bfloat16)
        to_ref[...] = select
        scaled = (factor * ref[:, :dcols].astype(jnp.float32)).astype(jnp.bfloat16)
        picked.append(lax.dot_general(select, scaled, TN, preferred_element_type=jnp.float32))
    slots = jnp.concatenate(picked, axis=0).astype(jnp.bfloat16)
    every_ref[first * capacity : (first + count) * capacity] = slots
    partial_ref[...] = lax.dot_general(
        slots, wdown_ref[...], NT, preferred_element_type=jnp.float32
    ).astype(jnp.bfloat16)


def take_rows(first, me, wdown, rows, every, total, experts):
    count, tok = len(rows), rows[0].shape[0]
    ff, dcols = wdown.shape
    capacity = total // experts
    smem = pl.BlockSpec(memory_space=pltpu.SMEM)
    old = [] if every is None else [every]
    lead = jax.ShapeDtypeStruct((tok, capacity), jnp.bfloat16)
    return pl.pallas_call(
        functools.partial(take_kernel, experts, count, first),
        in_specs=[smem] + [VMEM] * (1 + count + len(old)),
        out_specs=[VMEM] * (2 + count),
        out_shape=[
            pltpu.VMEM((total, dcols), jnp.bfloat16),
            jax.ShapeDtypeStruct((count * capacity, ff), jnp.bfloat16),
        ]
        + [lead] * count,
        input_output_aliases={2 + count: 0} if old else {},
        compiler_params=pltpu.CompilerParams(vmem_limit_bytes=14 << 20),
        cost_estimate=FREE,
        name="take",
    )(me, wdown, *rows, *old)


def give_kernel(count, first, mine_ref, theirs_ref, to_gate_ref, to_up_ref, wgate_ref, wup_ref, *refs):
    leads, outs = refs[:count], refs[count:]
    capacity = mine_ref.shape[0] // count
    span = slice(first * capacity, (first + count) * capacity)
    dh = mine_ref[...].astype(jnp.float32) + theirs_ref[...].astype(jnp.float32)
    dh = dh.astype(jnp.bfloat16).astype(jnp.float32)

    def scaled(ref):
        return (dh * ref[span].astype(jnp.float32)).astype(jnp.bfloat16)

    slot_grad = lax.dot_general(
        scaled(to_gate_ref), wgate_ref[...], NT, preferred_element_type=jnp.float32
    )
    slot_grad += lax.dot_general(
        scaled(to_up_ref), wup_ref[...], NT, preferred_element_type=jnp.float32
    )
    for i, (lead, out) in enumerate(zip(leads, outs)):
        part = slot_grad[i * capacity : (i + 1) * capacity].astype(jnp.bfloat16)
        out[...] = jnp.dot(lead[...], part, preferred_element_type=jnp.float32).astype(jnp.bfloat16)


def give_rows(first, mine, theirs, to_gate, to_up, wgate, wup, leads):
    count, tok = len(leads), leads[0].shape[0]
    out = jax.ShapeDtypeStruct((tok, wgate.shape[0]), jnp.bfloat16)
    return pl.pallas_call(
        functools.partial(give_kernel, count, first),
        in_specs=[VMEM] * (6 + count),
        out_specs=[VMEM] * count,
        out_shape=[out] * count,
        compiler_params=pltpu.CompilerParams(vmem_limit_bytes=16 << 20),
        cost_estimate=FREE,
        name="give",
    )(mine, theirs, to_gate, to_up, wgate, wup, *leads)


def add_kernel(span, own_ref, given_ref, *refs):
    out_ref = refs[-1]
    total = own_ref[:, span].astype(jnp.float32) + given_ref[:, span].astype(jnp.float32)
    if len(refs) > 1:
        received = jnp.concatenate([ref[...] for ref in refs[:-1]], axis=1)
        if received.shape != total.shape:
            received = received[:, span]
        total += received.astype(jnp.float32)
    out_ref[...] = total.astype(out_ref.dtype)


def add(span, own, given, received):
    parts = (own, given, *received)
    return pl.pallas_call(
        functools.partial(add_kernel, span),
        in_specs=[VMEM] * len(parts),
        out_specs=VMEM,
        out_shape=jax.ShapeDtypeStruct((own.shape[0], span.stop - span.start), own.dtype),
        compiler_params=pltpu.CompilerParams(vmem_limit_bytes=8 << 20),
        cost_estimate=FREE,
        name="add",
    )(*parts)


def grad_kernel(hidden_ref, every_ref, after_ref, *refs):
    refs[-1][...] = jnp.dot(
        hidden_ref[...], every_ref[...], preferred_element_type=jnp.float32
    ).astype(jnp.bfloat16)


def grad_rows(hidden, every, after, part, old):
    (ff, slots), dcols = hidden.shape, every.shape[1]
    rows = ff // 4
    return pl.pallas_call(
        grad_kernel,
        grid=(2,),
        in_specs=[pl.BlockSpec((rows, slots), lambda i: (2 * part + i, 0)), VMEM]
        + [ANY] * (1 + len(old)),
        out_specs=pl.BlockSpec((rows, dcols), lambda i: (2 * part + i, 0)),
        out_shape=jax.ShapeDtypeStruct((ff, dcols), jnp.bfloat16),
        input_output_aliases={3: 0} if old else {},
        compiler_params=pltpu.CompilerParams(vmem_limit_bytes=14 << 20),
        cost_estimate=FREE,
        name="grad_down",
    )(hidden, every, after, *old)


def mark(array, us):
    return pl.pallas_call(
        lambda old_ref, new_ref: None,
        in_specs=[ANY],
        out_specs=ANY,
        out_shape=jax.ShapeDtypeStruct(array.shape, array.dtype),
        input_output_aliases={0: 0},
        compiler_params=pltpu.CompilerParams(vmem_limit_bytes=1 << 20),
        cost_estimate=pl.CostEstimate(
            flops=int(us * 1.1e9), bytes_accessed=int(us * 3.6e6), transcendentals=0
        ),
        name="mark",
    )(array)


def mark(array, us):
    return pl.pallas_call(
        lambda old_ref, new_ref: None,
        in_specs=[ANY],
        out_specs=ANY,
        out_shape=jax.ShapeDtypeStruct(array.shape, array.dtype),
        input_output_aliases={0: 0},
        compiler_params=pltpu.CompilerParams(vmem_limit_bytes=1 << 20),
        cost_estimate=pl.CostEstimate(
            flops=int(us * 1.1e9), bytes_accessed=int(us * 3.6e6), transcendentals=0
        ),
        name="mark",
    )(array)


def sort_kernel(ids_ref, *refs):
    parts, out_ref, done = refs[:-2], refs[-2], refs[-1]
    copies, n = [], 0
    for part in parts:
        for i in range(part.shape[0]):
            copies.append(pltpu.make_async_copy(part.at[i], out_ref.at[ids_ref[n]], done.at[n]))
            n += 1
    for copy in copies:
        copy.start()
    for copy in copies:
        copy.wait()


def sort(ids, parts):
    groups = ids.shape[0]
    return pl.pallas_call(
        sort_kernel,
        in_specs=[pl.BlockSpec(memory_space=pltpu.SMEM)] + [ANY] * len(parts),
        out_specs=ANY,
        out_shape=jax.ShapeDtypeStruct((groups,) + parts[0].shape[1:], jnp.bfloat16),
        scratch_shapes=[pltpu.SemaphoreType.DMA((groups,))],
        compiler_params=pltpu.CompilerParams(vmem_limit_bytes=1 << 20),
        cost_estimate=FREE,
        name="sort",
    )(ids, *parts)


def ring_local(grad_out, routing, gates, scales, saved_gate, saved_up, w_gate, w_up, w_down):
    tok_rows, dcols = grad_out.shape
    groups = lax.axis_size("expert")
    slots = saved_gate.shape[2]
    capacity = slots // groups
    chips = groups // 2
    order = ring_of(chips)
    place = np.argsort(np.array(order))
    after = {order[i]: order[(i + 1) % chips] for i in range(chips)}
    ring = [(2 * j, 2 * after[j]) for j in range(chips)]
    ring += [(2 * after[j] + 1, 2 * j + 1) for j in range(chips)]
    sibling = [(i, i ^ 1) for i in range(groups)]
    swap = [(0, 1), (1, 0)]
    me = lax.axis_index("expert")
    back = [(b, a) for a, b in ring]
    stages = [(s, chips - s) for s in range(1, chips // 2)] + [(chips // 2,)]
    steps = [s for stage in stages for s in stage] + [0]
    table = np.zeros((groups, groups), np.int32)
    for device in range(groups):
        spot = place[device // 2]
        for i, step in enumerate(steps):
            down = 2 * order[(spot - step) % chips]
            up = 2 * order[(spot + step) % chips] + 1
            table[device, 2 * i : 2 * i + 2] = (down, up) if device % 2 == 0 else (up, down)
    ids = lax.dynamic_slice(jnp.asarray(table), (me, 0), (1, groups)).reshape(-1)
    me = me.reshape(1)

    payload = pack(grad_out, routing, gates, scales, groups)
    tiles = -(-saved_gate.shape[1] // LANES)
    *factors, token = prep(ids, saved_gate[0], saved_up[0], capacity, (0, SPLIT))
    wdown, _ = hold(w_down[0], token)

    tie = lax.optimization_barrier
    rows, others = {0: payload}, {}
    leads, partial, theirs, own, given, totals = {}, {}, {}, {}, {}, {}

    def pass_on(stage):
        for s in stage:
            if s <= chips // 2:
                rows[s] = lax.ppermute(rows[s - 1], "expert", ring)
            else:
                rows[s] = lax.ppermute(rows[(s + 1) % chips], "expert", back)

    def share(stage):
        for s in stage:
            others[s] = lax.ppermute(rows[s], "expert", sibling)

    def take(stage, every=None):
        near_far = [a for s in stage for a in (rows[s], others[s])]
        every, partial[stage], *leads[stage] = take_rows(
            2 * steps.index(stage[0]), me, wdown, near_far, every, slots, groups
        )
        return every

    def trade(stage):
        theirs[stage] = mark(lax.ppermute(partial[stage], "dp", swap), 10.0)

    def give(stage):
        first = 2 * steps.index(stage[0])
        parts = give_rows(
            first, partial[stage], theirs[stage], to_gate, to_up, *held, leads[stage]
        )
        for i, s in enumerate(stage):
            own[s] = parts[2 * i]
            given[s] = lax.ppermute(parts[2 * i + 1], "expert", sibling)

    def collect(s, before):
        received = [] if before is None else totals[before]
        received = [mark(lax.ppermute(part, "expert", ring), 8.0) for part in received]
        pieces = 2 if s >= HALVES else 1
        width = dcols // pieces
        totals[s] = []
        for p in range(pieces):
            mine = received[p : p + 1] if len(received) == pieces else received
            span = slice(p * width, (p + 1) * width)
            totals[s].append(add(span, own[s], given[s], mine))

    def after(values, keys, guard, key):
        *kept, guard[key] = tie(tuple(values[k] for k in keys) + (guard[key],))
        for k, v in zip(keys, kept):
            values[k] = v

    last = (0,)
    pass_on(stages[0])
    share(last)
    every = take(last)
    trade(last)
    after(rows, stages[0], partial, last)
    before = last
    for i, stage in enumerate(stages):
        final = i + 1 == len(stages)
        if not final:
            pass_on(stages[i + 1])
        share(stage)
        every = take(stage, every)
        trade(stage)
        if i == 0:
            ids, partial[stage] = tie((ids, partial[stage]))
            to_gate, to_up, hidden, token = prep(
                ids, saved_gate[0], saved_up[0], capacity, (SPLIT, tiles), factors
            )
            wgate, token = hold(w_gate[0], token)
            tokens = [token]
            after(rows, stages[1], tokens, 0)
        else:
            if i == 1:
                wup, _ = hold(w_up[0], leads[stage][0], *tokens)
                held = (wgate, wup)
            after(theirs, [before], partial, stage)
            give(before)
            if not final:
                after(rows, stages[i + 1], own, before[0])
            if i == 2:
                after(theirs, [last], own, before[0])
                give(last)
                after(given, [before[0]], own, 0)
            collect(before[0], before[0] - 1 if before[0] > 1 else None)
        before = stage
    after(theirs, [before], totals[before[0] - 1], 0)
    give(before)
    grads = [grad_rows(hidden, every, own[before[0]], 0, [])]
    after(given, [before[0]], grads, 0)
    for s in range(before[0], chips):
        collect(s, s - 1)
    grads = [grad_rows(hidden, every, totals[chips - 1][0], 1, grads)]
    received = [mark(lax.ppermute(part, "expert", ring), 8.0) for part in totals[chips - 1]]
    grad_x = add(slice(0, dcols), own[0], given[0], received)
    (grad_down,) = grads
    return (grad_x, grad_down[None])


def solution(mesh):
    paired = mesh.shape["dp"] == 2 and mesh.shape["expert"] % 4 == 0
    return jax.shard_map(
        ring_local if paired else exchange_local,
        mesh=mesh,
        in_specs=(
            P("expert", "dp"),
            P("expert", None),
            P("expert", None),
            P("expert"),
            P("expert", None, None),
            P("expert", None, None),
            P("expert", "dp", None),
            P("expert", "dp", None),
            P("expert", None, "dp"),
        ),
        out_specs=(P("expert", "dp"), P("expert", None, "dp")),
        check_vma=False,
    )
```

```python
import functools

import jax
import jax.numpy as jnp
import numpy as np
from jax import lax
from jax.experimental import pallas as pl
from jax.experimental.pallas import tpu as pltpu
from jax.sharding import PartitionSpec as P

LANES = 128
PIECES = 4
HALVES = 4
SPLIT = 6
NT = (((1,), (1,)), ((), ()))
TN = (((0,), (0,)), ((), ()))
VMEM = pl.BlockSpec(memory_space=pltpu.VMEM)
ANY = pl.BlockSpec(memory_space=pl.ANY)
TOKEN = jax.ShapeDtypeStruct((8, LANES), jnp.float32)
FREE = pl.CostEstimate(flops=0, bytes_accessed=0, transcendentals=0)


def activation_grad(hidden_grad, gate_pre, up_pre):
    g = gate_pre.astype(jnp.float32)
    u = up_pre.astype(jnp.float32)
    sig = jax.nn.sigmoid(g)
    dh = hidden_grad.astype(jnp.float32)
    gate_grad = (dh * u * sig * (1.0 + g * (1.0 - sig))).astype(jnp.bfloat16)
    up_grad = (dh * g * sig).astype(jnp.bfloat16)
    return (gate_grad, up_grad)


def contract(left, weights):
    return lax.dot_general(
        left, weights, (((0,), (1,)), ((), ())), preferred_element_type=jnp.float32
    )


def exchange_local(grad_out, routing, gates, scales, saved_gate, saved_up, w_gate, w_up, w_down):
    tok_rows, dcols = grad_out.shape
    topk = routing.shape[1]
    groups = lax.axis_size("expert")
    experts = groups * w_gate.shape[0]
    slots = saved_gate.shape[2]
    capacity = slots // groups
    flat_route = routing.reshape(-1)
    hot = (flat_route[:, None] == jnp.arange(experts, dtype=jnp.int32)[None, :]).astype(jnp.int32)
    position = jnp.sum(hot * (jnp.cumsum(hot, axis=0) - 1), axis=1)
    target = flat_route * capacity + position
    select = jnp.arange(experts * capacity, dtype=jnp.int32)[:, None] == target[None, :]
    weight = (gates * scales[:, None]).reshape(-1)
    slot_factor = jnp.sum(jnp.where(select, weight[None, :], 0.0), axis=1)
    collect = jnp.any(select.reshape(experts * capacity, tok_rows, topk), axis=2).astype(
        jnp.bfloat16
    )
    owned_rows = jnp.dot(collect, grad_out, preferred_element_type=jnp.float32)
    sending = (
        (slot_factor[:, None] * owned_rows).astype(jnp.bfloat16).reshape(experts, capacity, dcols)
    )
    arrived = lax.all_to_all(sending, "expert", split_axis=0, concat_axis=0, tiled=True).reshape(
        slots, dcols
    )
    wdown = w_down[0]
    wgate = w_gate[0]
    wup = w_up[0]
    sgate = saved_gate[0]
    sup = saved_up[0]
    partial_value = lax.dot_general(
        wdown, arrived, (((1,), (1,)), ((), ())), preferred_element_type=jnp.float32
    )
    reduced = lax.psum_scatter(
        partial_value.astype(jnp.bfloat16), "dp", scatter_dimension=0, tiled=True
    )
    hidden_grad = lax.all_gather(reduced, "dp", axis=0, tiled=True)
    gate_grad, up_grad = activation_grad(hidden_grad, sgate, sup)
    slot_grad = contract(gate_grad, wgate) + contract(up_grad, wup)
    gate_full = sgate.astype(jnp.float32)
    hidden = (gate_full * jax.nn.sigmoid(gate_full) * sup.astype(jnp.float32)).astype(jnp.bfloat16)
    grad_down = jnp.dot(hidden, arrived, preferred_element_type=jnp.float32).astype(jnp.bfloat16)
    returning = slot_grad.astype(jnp.bfloat16).reshape(groups, capacity, dcols)
    back = lax.all_to_all(returning, "expert", split_axis=0, concat_axis=0, tiled=True).reshape(
        experts * capacity, dcols
    )
    grad_x = lax.dot_general(
        collect, back, (((0,), (0,)), ((), ())), preferred_element_type=jnp.float32
    )
    return (grad_x.astype(jnp.bfloat16), grad_down[None])


def ring_of(chips):
    return list(range(0, chips, 2)) + list(range(1, chips, 2))[::-1]


def pack_kernel(experts, rows_ref, routing_ref, gates_ref, scales_ref, out_ref):
    topk, tok = routing_ref.shape
    dcols = rows_ref.shape[1]
    lanes = out_ref.shape[1] - dcols
    out_ref[:, :dcols] = rows_ref[...]
    line = lax.broadcasted_iota(jnp.int32, (lanes, tok), 0)
    expert = line % experts
    piece = line // experts
    hot = jnp.zeros((lanes, tok), jnp.float32)
    factor = jnp.zeros((lanes, tok), jnp.float32)
    for k in range(topk):
        same = routing_ref[k : k + 1] == expert
        hot += jnp.where(same, 1.0, 0.0)
        factor += jnp.where(same, gates_ref[k : k + 1] * scales_ref[...], 0.0)
    row = lax.broadcasted_iota(jnp.int32, (tok, tok), 0)
    column = lax.broadcasted_iota(jnp.int32, (tok, tok), 1)
    earlier = jnp.where(row < column, 1.0, 0.0).astype(jnp.bfloat16)
    before = jnp.dot(hot.astype(jnp.bfloat16), earlier, preferred_element_type=jnp.float32)
    high = factor.astype(jnp.bfloat16)
    rest = factor - high.astype(jnp.float32)
    middle = rest.astype(jnp.bfloat16)
    low = rest - middle.astype(jnp.float32)
    meta = jnp.where(piece == 0, hot * (before + 1.0), 0.0)
    meta = jnp.where(piece == 1, high.astype(jnp.float32), meta)
    meta = jnp.where(piece == 2, middle.astype(jnp.float32), meta)
    meta = jnp.where(piece == 3, low, meta)
    out_ref[:, dcols:] = meta.T.astype(jnp.bfloat16)


def whole(shape):
    return pl.BlockSpec(shape, lambda i: (0,) * len(shape))


def pack(rows, routing, gates, scales, experts):
    tok, dcols = rows.shape
    lanes = -(-PIECES * experts // LANES) * LANES
    operands = [
        pltpu.with_memory_space_constraint(a, pltpu.HBM)
        for a in (rows, routing.T, gates.T, scales[None])
    ]
    return pl.pallas_call(
        functools.partial(pack_kernel, experts),
        grid=(1,),
        in_specs=[whole(a.shape) for a in operands],
        out_specs=whole((tok, dcols + lanes)),
        out_shape=jax.ShapeDtypeStruct((tok, dcols + lanes), jnp.bfloat16),
        compiler_params=pltpu.CompilerParams(vmem_limit_bytes=8 << 20),
        cost_estimate=FREE,
        name="pack",
    )(*operands)


def prep_kernel(capacity, first, ids_ref, gate_ref, up_ref, *refs):
    to_gate_ref, to_up_ref, hidden_ref, token_ref, turned = refs[-5:]
    g = gate_ref[...].astype(jnp.float32)
    u = up_ref[...].astype(jnp.float32)
    sig = jax.nn.sigmoid(g)
    swish = g * sig
    turned[0] = (u * sig * (1.0 + g * (1.0 - sig))).T
    turned[1] = swish.T
    turned[2] = (swish * u).T

    def in_order(k):
        groups = gate_ref.shape[1] // capacity
        starts = [pl.multiple_of(ids_ref[i] * capacity, 8) for i in range(groups)]
        return jnp.concatenate([turned[k, pl.ds(start, capacity)] for start in starts], axis=0)

    span = pl.ds(pl.multiple_of((first + pl.program_id(0)) * LANES, LANES), LANES)
    to_gate_ref[:, span] = in_order(0).astype(jnp.bfloat16)
    to_up_ref[:, span] = in_order(1).astype(jnp.bfloat16)
    hidden_ref[span] = in_order(2).T.astype(jnp.bfloat16)
    token_ref[...] = jnp.zeros(token_ref.shape, token_ref.dtype)


def prep(ids, gate, up, capacity, tiles, old=()):
    ff, slots = gate.shape
    spec = pl.BlockSpec((LANES, slots), lambda i, ids: (tiles[0] + i, 0))
    operands = [pltpu.with_memory_space_constraint(a, pltpu.HBM) for a in (gate, up)]
    count = (tiles[1] - tiles[0]) * LANES
    return pl.pallas_call(
        functools.partial(prep_kernel, capacity, tiles[0]),
        grid_spec=pltpu.PrefetchScalarGridSpec(
            num_scalar_prefetch=1,
            grid=(tiles[1] - tiles[0],),
            in_specs=[spec, spec] + [VMEM] * len(old),
            out_specs=[VMEM] * 3 + [pl.BlockSpec(TOKEN.shape, lambda i, ids: (0, 0))],
            scratch_shapes=[pltpu.VMEM((3, slots, LANES), jnp.float32)],
        ),
        out_shape=[
            pltpu.VMEM((slots, ff), jnp.bfloat16),
            pltpu.VMEM((slots, ff), jnp.bfloat16),
            pltpu.VMEM((ff, slots), jnp.bfloat16),
            TOKEN,
        ],
        input_output_aliases={3 + i: i for i in range(len(old))},
        compiler_params=pltpu.CompilerParams(vmem_limit_bytes=8 << 20),
        cost_estimate=pl.CostEstimate(
            flops=10 * count * slots, bytes_accessed=10 * count * slots, transcendentals=count * slots
        ),
        name="prep",
    )(ids, *operands, *old)


def hold_kernel(weights_ref, *refs):
    out_ref, token_ref, done = refs[-3:]
    copy = pltpu.make_async_copy(weights_ref, out_ref, done)
    copy.start()
    token_ref[...] = jnp.zeros(token_ref.shape, token_ref.dtype)
    copy.wait()


def hold(weights, *after):
    return pl.pallas_call(
        hold_kernel,
        in_specs=[ANY] * (1 + len(after)),
        out_specs=[VMEM, VMEM],
        out_shape=[pltpu.VMEM(weights.shape, weights.dtype), TOKEN],
        scratch_shapes=[pltpu.SemaphoreType.DMA(())],
        compiler_params=pltpu.CompilerParams(vmem_limit_bytes=1 << 20),
        cost_estimate=FREE,
        name="hold",
    )(pltpu.with_memory_space_constraint(weights, pltpu.HBM), *after)


def take_kernel(experts, count, first, me_ref, wdown_ref, *refs):
    rows, (every_ref, partial_ref, *leads) = refs[:count], refs[-2 - count :]
    dcols = every_ref.shape[1]
    capacity = every_ref.shape[0] // experts
    me = me_ref[0]
    picked = []
    for ref, to_ref in zip(rows, leads):
        meta = ref[:, dcols:].astype(jnp.float32)
        tok, lanes = meta.shape
        lane = lax.broadcasted_iota(jnp.int32, (tok, lanes), 1)
        mine = lane % experts == me
        places = jnp.where(mine & (lane < experts), meta, 0.0)
        share = jnp.where(mine & (lane >= experts), meta, 0.0)
        position = jnp.sum(places, axis=1, keepdims=True) - 1.0
        factor = jnp.sum(share, axis=1, keepdims=True)
        slot = lax.broadcasted_iota(jnp.int32, (tok, capacity), 1).astype(jnp.float32)
        select = jnp.where(slot == position, 1.0, 0.0).astype(jnp.bfloat16)
        to_ref[...] = select
        scaled = (factor * ref[:, :dcols].astype(jnp.float32)).astype(jnp.bfloat16)
        picked.append(lax.dot_general(select, scaled, TN, preferred_element_type=jnp.float32))
    slots = jnp.concatenate(picked, axis=0).astype(jnp.bfloat16)
    every_ref[first * capacity : (first + count) * capacity] = slots
    partial_ref[...] = lax.dot_general(
        slots, wdown_ref[...], NT, preferred_element_type=jnp.float32
    ).astype(jnp.bfloat16)


def take_rows(first, me, wdown, rows, every, total, experts):
    count, tok = len(rows), rows[0].shape[0]
    ff, dcols = wdown.shape
    capacity = total // experts
    smem = pl.BlockSpec(memory_space=pltpu.SMEM)
    old = [] if every is None else [every]
    lead = jax.ShapeDtypeStruct((tok, capacity), jnp.bfloat16)
    return pl.pallas_call(
        functools.partial(take_kernel, experts, count, first),
        in_specs=[smem] + [VMEM] * (1 + count + len(old)),
        out_specs=[VMEM] * (2 + count),
        out_shape=[
            pltpu.VMEM((total, dcols), jnp.bfloat16),
            jax.ShapeDtypeStruct((count * capacity, ff), jnp.bfloat16),
        ]
        + [lead] * count,
        input_output_aliases={2 + count: 0} if old else {},
        compiler_params=pltpu.CompilerParams(vmem_limit_bytes=14 << 20),
        cost_estimate=FREE,
        name="take",
    )(me, wdown, *rows, *old)


def give_kernel(count, first, mine_ref, theirs_ref, to_gate_ref, to_up_ref, wgate_ref, wup_ref, *refs):
    leads, outs = refs[:count], refs[count:]
    capacity = mine_ref.shape[0] // count
    span = slice(first * capacity, (first + count) * capacity)
    dh = mine_ref[...].astype(jnp.float32) + theirs_ref[...].astype(jnp.float32)
    dh = dh.astype(jnp.bfloat16).astype(jnp.float32)

    def scaled(ref):
        return (dh * ref[span].astype(jnp.float32)).astype(jnp.bfloat16)

    slot_grad = lax.dot_general(
        scaled(to_gate_ref), wgate_ref[...], NT, preferred_element_type=jnp.float32
    )
    slot_grad += lax.dot_general(
        scaled(to_up_ref), wup_ref[...], NT, preferred_element_type=jnp.float32
    )
    for i, (lead, out) in enumerate(zip(leads, outs)):
        part = slot_grad[i * capacity : (i + 1) * capacity].astype(jnp.bfloat16)
        out[...] = jnp.dot(lead[...], part, preferred_element_type=jnp.float32).astype(jnp.bfloat16)


def give_rows(first, mine, theirs, to_gate, to_up, wgate, wup, leads):
    count, tok = len(leads), leads[0].shape[0]
    out = jax.ShapeDtypeStruct((tok, wgate.shape[0]), jnp.bfloat16)
    return pl.pallas_call(
        functools.partial(give_kernel, count, first),
        in_specs=[VMEM] * (6 + count),
        out_specs=[VMEM] * count,
        out_shape=[out] * count,
        compiler_params=pltpu.CompilerParams(vmem_limit_bytes=16 << 20),
        cost_estimate=FREE,
        name="give",
    )(mine, theirs, to_gate, to_up, wgate, wup, *leads)


def add_kernel(span, own_ref, given_ref, *refs):
    out_ref = refs[-1]
    total = own_ref[:, span].astype(jnp.float32) + given_ref[:, span].astype(jnp.float32)
    if len(refs) > 1:
        received = jnp.concatenate([ref[...] for ref in refs[:-1]], axis=1)
        if received.shape != total.shape:
            received = received[:, span]
        total += received.astype(jnp.float32)
    out_ref[...] = total.astype(out_ref.dtype)


def add(span, own, given, received):
    parts = (own, given, *received)
    return pl.pallas_call(
        functools.partial(add_kernel, span),
        in_specs=[VMEM] * len(parts),
        out_specs=VMEM,
        out_shape=jax.ShapeDtypeStruct((own.shape[0], span.stop - span.start), own.dtype),
        compiler_params=pltpu.CompilerParams(vmem_limit_bytes=8 << 20),
        cost_estimate=FREE,
        name="add",
    )(*parts)


def grad_kernel(hidden_ref, every_ref, after_ref, *refs):
    refs[-1][...] = jnp.dot(
        hidden_ref[...], every_ref[...], preferred_element_type=jnp.float32
    ).astype(jnp.bfloat16)


def grad_rows(hidden, every, after, part, old):
    (ff, slots), dcols = hidden.shape, every.shape[1]
    rows = ff // 4
    return pl.pallas_call(
        grad_kernel,
        grid=(2,),
        in_specs=[pl.BlockSpec((rows, slots), lambda i: (2 * part + i, 0)), VMEM]
        + [ANY] * (1 + len(old)),
        out_specs=pl.BlockSpec((rows, dcols), lambda i: (2 * part + i, 0)),
        out_shape=jax.ShapeDtypeStruct((ff, dcols), jnp.bfloat16),
        input_output_aliases={3: 0} if old else {},
        compiler_params=pltpu.CompilerParams(vmem_limit_bytes=14 << 20),
        cost_estimate=FREE,
        name="grad_down",
    )(hidden, every, after, *old)


def mark(array, us):
    return pl.pallas_call(
        lambda old_ref, new_ref: None,
        in_specs=[ANY],
        out_specs=ANY,
        out_shape=jax.ShapeDtypeStruct(array.shape, array.dtype),
        input_output_aliases={0: 0},
        compiler_params=pltpu.CompilerParams(vmem_limit_bytes=1 << 20),
        cost_estimate=pl.CostEstimate(
            flops=int(us * 1.1e9), bytes_accessed=int(us * 3.6e6), transcendentals=0
        ),
        name="mark",
    )(array)


def mark(array, us):
    return pl.pallas_call(
        lambda old_ref, new_ref: None,
        in_specs=[ANY],
        out_specs=ANY,
        out_shape=jax.ShapeDtypeStruct(array.shape, array.dtype),
        input_output_aliases={0: 0},
        compiler_params=pltpu.CompilerParams(vmem_limit_bytes=1 << 20),
        cost_estimate=pl.CostEstimate(
            flops=int(us * 1.1e9), bytes_accessed=int(us * 3.6e6), transcendentals=0
        ),
        name="mark",
    )(array)


def sort_kernel(ids_ref, *refs):
    parts, out_ref, done = refs[:-2], refs[-2], refs[-1]
    copies, n = [], 0
    for part in parts:
        for i in range(part.shape[0]):
            copies.append(pltpu.make_async_copy(part.at[i], out_ref.at[ids_ref[n]], done.at[n]))
            n += 1
    for copy in copies:
        copy.start()
    for copy in copies:
        copy.wait()


def sort(ids, parts):
    groups = ids.shape[0]
    return pl.pallas_call(
        sort_kernel,
        in_specs=[pl.BlockSpec(memory_space=pltpu.SMEM)] + [ANY] * len(parts),
        out_specs=ANY,
        out_shape=jax.ShapeDtypeStruct((groups,) + parts[0].shape[1:], jnp.bfloat16),
        scratch_shapes=[pltpu.SemaphoreType.DMA((groups,))],
        compiler_params=pltpu.CompilerParams(vmem_limit_bytes=1 << 20),
        cost_estimate=FREE,
        name="sort",
    )(ids, *parts)


def ring_local(grad_out, routing, gates, scales, saved_gate, saved_up, w_gate, w_up, w_down):
    tok_rows, dcols = grad_out.shape
    groups = lax.axis_size("expert")
    slots = saved_gate.shape[2]
    capacity = slots // groups
    chips = groups // 2
    order = ring_of(chips)
    place = np.argsort(np.array(order))
    after = {order[i]: order[(i + 1) % chips] for i in range(chips)}
    ring = [(2 * j, 2 * after[j]) for j in range(chips)]
    ring += [(2 * after[j] + 1, 2 * j + 1) for j in range(chips)]
    sibling = [(i, i ^ 1) for i in range(groups)]
    swap = [(0, 1), (1, 0)]
    me = lax.axis_index("expert")
    back = [(b, a) for a, b in ring]
    stages = [(s, chips - s) for s in range(1, chips // 2)] + [(chips // 2,)]
    steps = [s for stage in stages for s in stage] + [0]
    table = np.zeros((groups, groups), np.int32)
    for device in range(groups):
        spot = place[device // 2]
        for i, step in enumerate(steps):
            down = 2 * order[(spot - step) % chips]
            up = 2 * order[(spot + step) % chips] + 1
            table[device, 2 * i : 2 * i + 2] = (down, up) if device % 2 == 0 else (up, down)
    ids = lax.dynamic_slice(jnp.asarray(table), (me, 0), (1, groups)).reshape(-1)
    me = me.reshape(1)

    payload = pack(grad_out, routing, gates, scales, groups)
    tiles = -(-saved_gate.shape[1] // LANES)
    wdown, _ = hold(w_down[0], payload, ids)

    tie = lax.optimization_barrier
    rows, others = {0: payload}, {}
    leads, partial, theirs, own, given, totals = {}, {}, {}, {}, {}, {}

    def pass_on(stage):
        for s in stage:
            if s <= chips // 2:
                rows[s] = lax.ppermute(rows[s - 1], "expert", ring)
            else:
                rows[s] = lax.ppermute(rows[(s + 1) % chips], "expert", back)

    def share(stage):
        for s in stage:
            others[s] = lax.ppermute(rows[s], "expert", sibling)

    def take(stage, every=None):
        near_far = [a for s in stage for a in (rows[s], others[s])]
        every, partial[stage], *leads[stage] = take_rows(
            2 * steps.index(stage[0]), me, wdown, near_far, every, slots, groups
        )
        return every

    def trade(stage):
        theirs[stage] = lax.ppermute(partial[stage], "dp", swap)

    def give(stage, marked=False):
        first = 2 * steps.index(stage[0])
        there = theirs[stage] if marked else mark(theirs[stage], 10.0)
        parts = give_rows(
            first, partial[stage], there, to_gate, to_up, *held, leads[stage]
        )
        for i, s in enumerate(stage):
            own[s] = parts[2 * i]
            given[s] = lax.ppermute(parts[2 * i + 1], "expert", sibling)

    def collect(s, before):
        received = [] if before is None else totals[before]
        estimate = 8.0 if s <= HALVES else 1.0
        received = [mark(lax.ppermute(part, "expert", ring), estimate) for part in received]
        if s == HALVES:
            received = [mark(part, 8.0) for part in received]
        pieces = 2 if s >= HALVES else 1
        width = dcols // pieces
        totals[s] = []
        for p in range(pieces):
            mine = received[p : p + 1] if len(received) == pieces else received
            span = slice(p * width, (p + 1) * width)
            totals[s].append(add(span, own[s], given[s], mine))

    def after(values, keys, guard, key):
        *kept, guard[key] = tie(tuple(values[k] for k in keys) + (guard[key],))
        for k, v in zip(keys, kept):
            values[k] = v

    last = (0,)
    pass_on(stages[0])
    share(last)
    every = take(last)
    ids, partial[last] = tie((ids, partial[last]))
    *factors, token = prep(ids, saved_gate[0], saved_up[0], capacity, (0, SPLIT))
    rows[1], early = tie((rows[1], token))
    after(rows, stages[0], partial, last)
    before = last
    for i, stage in enumerate(stages):
        final = i + 1 == len(stages)
        if not final:
            pass_on(stages[i + 1])
        share(stage)
        every = take(stage, every)
        trade(stage)
        if i == 0:
            ids, partial[stage] = tie((ids, partial[stage]))
            to_gate, to_up, hidden, token = prep(
                ids, saved_gate[0], saved_up[0], capacity, (SPLIT, tiles), factors
            )
            wgate, token = hold(w_gate[0], early, token)
            tokens = [token]
            after(rows, stages[1], tokens, 0)
        else:
            if i == 1:
                wup, _ = hold(w_up[0], leads[stage][0], *tokens)
                held = (wgate, wup)
            after(theirs, [before], partial, stage)
            if i + 1 == len(stages):
                grads = [grad_rows(hidden, every, leads[stage][0], 0, [])]
                after(theirs, [before], grads, 0)
            give(before)
            if not final:
                after(rows, stages[i + 1], own, before[0])
            collect(before[0], before[0] - 1 if before[0] > 1 else None)
        before = stage
    after(theirs, [before], totals[before[0] - 1], 0)
    after(partial, [last], totals[before[0] - 1], 0)
    trade(last)
    give(before)
    for s in range(before[0], chips):
        collect(s, s - 1)
        if s == before[0] + 1:
            after(theirs, [last], totals[s], 1)
            give(last)
            after(given, [s + 1], own, 0)
    grads = [grad_rows(hidden, every, totals[chips - 1][0], 1, grads)]
    received = [mark(lax.ppermute(part, "expert", ring), 1.0) for part in totals[chips - 1]]
    grad_x = add(slice(0, dcols), own[0], given[0], received)
    (grad_down,) = grads
    return (grad_x, grad_down[None])


def solution(mesh):
    paired = mesh.shape["dp"] == 2 and mesh.shape["expert"] % 4 == 0
    return jax.shard_map(
        ring_local if paired else exchange_local,
        mesh=mesh,
        in_specs=(
            P("expert", "dp"),
            P("expert", None),
            P("expert", None),
            P("expert"),
            P("expert", None, None),
            P("expert", None, None),
            P("expert", "dp", None),
            P("expert", "dp", None),
            P("expert", None, "dp"),
        ),
        out_specs=(P("expert", "dp"), P("expert", None, "dp")),
        check_vma=False,
    )
```

```python
import functools

import jax
import jax.numpy as jnp
import numpy as np
from jax import lax
from jax.experimental import pallas as pl
from jax.experimental.pallas import tpu as pltpu
from jax.sharding import PartitionSpec as P

LANES = 128
PIECES = 4
HALVES = 4
SPLIT = 6
NT = (((1,), (1,)), ((), ()))
TN = (((0,), (0,)), ((), ()))
VMEM = pl.BlockSpec(memory_space=pltpu.VMEM)
ANY = pl.BlockSpec(memory_space=pl.ANY)
TOKEN = jax.ShapeDtypeStruct((8, LANES), jnp.float32)
FREE = pl.CostEstimate(flops=0, bytes_accessed=0, transcendentals=0)


def activation_grad(hidden_grad, gate_pre, up_pre):
    g = gate_pre.astype(jnp.float32)
    u = up_pre.astype(jnp.float32)
    sig = jax.nn.sigmoid(g)
    dh = hidden_grad.astype(jnp.float32)
    gate_grad = (dh * u * sig * (1.0 + g * (1.0 - sig))).astype(jnp.bfloat16)
    up_grad = (dh * g * sig).astype(jnp.bfloat16)
    return (gate_grad, up_grad)


def contract(left, weights):
    return lax.dot_general(
        left, weights, (((0,), (1,)), ((), ())), preferred_element_type=jnp.float32
    )


def exchange_local(grad_out, routing, gates, scales, saved_gate, saved_up, w_gate, w_up, w_down):
    tok_rows, dcols = grad_out.shape
    topk = routing.shape[1]
    groups = lax.axis_size("expert")
    experts = groups * w_gate.shape[0]
    slots = saved_gate.shape[2]
    capacity = slots // groups
    flat_route = routing.reshape(-1)
    hot = (flat_route[:, None] == jnp.arange(experts, dtype=jnp.int32)[None, :]).astype(jnp.int32)
    position = jnp.sum(hot * (jnp.cumsum(hot, axis=0) - 1), axis=1)
    target = flat_route * capacity + position
    select = jnp.arange(experts * capacity, dtype=jnp.int32)[:, None] == target[None, :]
    weight = (gates * scales[:, None]).reshape(-1)
    slot_factor = jnp.sum(jnp.where(select, weight[None, :], 0.0), axis=1)
    collect = jnp.any(select.reshape(experts * capacity, tok_rows, topk), axis=2).astype(
        jnp.bfloat16
    )
    owned_rows = jnp.dot(collect, grad_out, preferred_element_type=jnp.float32)
    sending = (
        (slot_factor[:, None] * owned_rows).astype(jnp.bfloat16).reshape(experts, capacity, dcols)
    )
    arrived = lax.all_to_all(sending, "expert", split_axis=0, concat_axis=0, tiled=True).reshape(
        slots, dcols
    )
    wdown = w_down[0]
    wgate = w_gate[0]
    wup = w_up[0]
    sgate = saved_gate[0]
    sup = saved_up[0]
    partial_value = lax.dot_general(
        wdown, arrived, (((1,), (1,)), ((), ())), preferred_element_type=jnp.float32
    )
    reduced = lax.psum_scatter(
        partial_value.astype(jnp.bfloat16), "dp", scatter_dimension=0, tiled=True
    )
    hidden_grad = lax.all_gather(reduced, "dp", axis=0, tiled=True)
    gate_grad, up_grad = activation_grad(hidden_grad, sgate, sup)
    slot_grad = contract(gate_grad, wgate) + contract(up_grad, wup)
    gate_full = sgate.astype(jnp.float32)
    hidden = (gate_full * jax.nn.sigmoid(gate_full) * sup.astype(jnp.float32)).astype(jnp.bfloat16)
    grad_down = jnp.dot(hidden, arrived, preferred_element_type=jnp.float32).astype(jnp.bfloat16)
    returning = slot_grad.astype(jnp.bfloat16).reshape(groups, capacity, dcols)
    back = lax.all_to_all(returning, "expert", split_axis=0, concat_axis=0, tiled=True).reshape(
        experts * capacity, dcols
    )
    grad_x = lax.dot_general(
        collect, back, (((0,), (0,)), ((), ())), preferred_element_type=jnp.float32
    )
    return (grad_x.astype(jnp.bfloat16), grad_down[None])


def ring_of(chips):
    return list(range(0, chips, 2)) + list(range(1, chips, 2))[::-1]


def pack_kernel(experts, rows_ref, routing_ref, gates_ref, scales_ref, out_ref):
    topk, tok = routing_ref.shape
    dcols = rows_ref.shape[1]
    lanes = out_ref.shape[1] - dcols
    out_ref[:, :dcols] = rows_ref[...]
    line = lax.broadcasted_iota(jnp.int32, (lanes, tok), 0)
    expert = line % experts
    piece = line // experts
    hot = jnp.zeros((lanes, tok), jnp.float32)
    factor = jnp.zeros((lanes, tok), jnp.float32)
    for k in range(topk):
        same = routing_ref[k : k + 1] == expert
        hot += jnp.where(same, 1.0, 0.0)
        factor += jnp.where(same, gates_ref[k : k + 1] * scales_ref[...], 0.0)
    row = lax.broadcasted_iota(jnp.int32, (tok, tok), 0)
    column = lax.broadcasted_iota(jnp.int32, (tok, tok), 1)
    earlier = jnp.where(row < column, 1.0, 0.0).astype(jnp.bfloat16)
    before = jnp.dot(hot.astype(jnp.bfloat16), earlier, preferred_element_type=jnp.float32)
    high = factor.astype(jnp.bfloat16)
    rest = factor - high.astype(jnp.float32)
    middle = rest.astype(jnp.bfloat16)
    low = rest - middle.astype(jnp.float32)
    meta = jnp.where(piece == 0, hot * (before + 1.0), 0.0)
    meta = jnp.where(piece == 1, high.astype(jnp.float32), meta)
    meta = jnp.where(piece == 2, middle.astype(jnp.float32), meta)
    meta = jnp.where(piece == 3, low, meta)
    out_ref[:, dcols:] = meta.T.astype(jnp.bfloat16)


def whole(shape):
    return pl.BlockSpec(shape, lambda i: (0,) * len(shape))


def pack(rows, routing, gates, scales, experts):
    tok, dcols = rows.shape
    lanes = -(-PIECES * experts // LANES) * LANES
    operands = [
        pltpu.with_memory_space_constraint(a, pltpu.HBM)
        for a in (rows, routing.T, gates.T, scales[None])
    ]
    return pl.pallas_call(
        functools.partial(pack_kernel, experts),
        grid=(1,),
        in_specs=[whole(a.shape) for a in operands],
        out_specs=whole((tok, dcols + lanes)),
        out_shape=jax.ShapeDtypeStruct((tok, dcols + lanes), jnp.bfloat16),
        compiler_params=pltpu.CompilerParams(vmem_limit_bytes=8 << 20),
        cost_estimate=FREE,
        name="pack",
    )(*operands)


def prep_kernel(capacity, first, ids_ref, gate_ref, up_ref, *refs):
    to_gate_ref, to_up_ref, hidden_ref, token_ref, turned = refs[-5:]
    g = gate_ref[...].astype(jnp.float32)
    u = up_ref[...].astype(jnp.float32)
    sig = jax.nn.sigmoid(g)
    swish = g * sig
    turned[0] = (u * sig * (1.0 + g * (1.0 - sig))).T
    turned[1] = swish.T
    turned[2] = (swish * u).T

    def in_order(k):
        groups = gate_ref.shape[1] // capacity
        starts = [pl.multiple_of(ids_ref[i] * capacity, 8) for i in range(groups)]
        return jnp.concatenate([turned[k, pl.ds(start, capacity)] for start in starts], axis=0)

    span = pl.ds(pl.multiple_of((first + pl.program_id(0)) * LANES, LANES), LANES)
    to_gate_ref[:, span] = in_order(0).astype(jnp.bfloat16)
    to_up_ref[:, span] = in_order(1).astype(jnp.bfloat16)
    hidden_ref[span] = in_order(2).T.astype(jnp.bfloat16)
    token_ref[...] = jnp.zeros(token_ref.shape, token_ref.dtype)


def prep(ids, gate, up, capacity, tiles, old=()):
    ff, slots = gate.shape
    spec = pl.BlockSpec((LANES, slots), lambda i, ids: (tiles[0] + i, 0))
    operands = [pltpu.with_memory_space_constraint(a, pltpu.HBM) for a in (gate, up)]
    count = (tiles[1] - tiles[0]) * LANES
    return pl.pallas_call(
        functools.partial(prep_kernel, capacity, tiles[0]),
        grid_spec=pltpu.PrefetchScalarGridSpec(
            num_scalar_prefetch=1,
            grid=(tiles[1] - tiles[0],),
            in_specs=[spec, spec] + [VMEM] * len(old),
            out_specs=[VMEM] * 3 + [pl.BlockSpec(TOKEN.shape, lambda i, ids: (0, 0))],
            scratch_shapes=[pltpu.VMEM((3, slots, LANES), jnp.float32)],
        ),
        out_shape=[
            pltpu.VMEM((slots, ff), jnp.bfloat16),
            pltpu.VMEM((slots, ff), jnp.bfloat16),
            pltpu.VMEM((ff, slots), jnp.bfloat16),
            TOKEN,
        ],
        input_output_aliases={3 + i: i for i in range(len(old))},
        compiler_params=pltpu.CompilerParams(vmem_limit_bytes=8 << 20),
        cost_estimate=pl.CostEstimate(
            flops=10 * count * slots, bytes_accessed=10 * count * slots, transcendentals=count * slots
        ),
        name="prep",
    )(ids, *operands, *old)


def hold_kernel(weights_ref, *refs):
    out_ref, token_ref, done = refs[-3:]
    copy = pltpu.make_async_copy(weights_ref, out_ref, done)
    copy.start()
    token_ref[...] = jnp.zeros(token_ref.shape, token_ref.dtype)
    copy.wait()


def hold(weights, *after):
    return pl.pallas_call(
        hold_kernel,
        in_specs=[ANY] * (1 + len(after)),
        out_specs=[VMEM, VMEM],
        out_shape=[pltpu.VMEM(weights.shape, weights.dtype), TOKEN],
        scratch_shapes=[pltpu.SemaphoreType.DMA(())],
        compiler_params=pltpu.CompilerParams(vmem_limit_bytes=1 << 20),
        cost_estimate=FREE,
        name="hold",
    )(pltpu.with_memory_space_constraint(weights, pltpu.HBM), *after)


def take_kernel(experts, count, first, me_ref, wdown_ref, *refs):
    rows, (every_ref, partial_ref, *leads) = refs[:count], refs[-2 - count :]
    dcols = every_ref.shape[1]
    capacity = every_ref.shape[0] // experts
    me = me_ref[0]
    picked = []
    for ref, to_ref in zip(rows, leads):
        meta = ref[:, dcols:].astype(jnp.float32)
        tok, lanes = meta.shape
        lane = lax.broadcasted_iota(jnp.int32, (tok, lanes), 1)
        mine = lane % experts == me
        places = jnp.where(mine & (lane < experts), meta, 0.0)
        share = jnp.where(mine & (lane >= experts), meta, 0.0)
        position = jnp.sum(places, axis=1, keepdims=True) - 1.0
        factor = jnp.sum(share, axis=1, keepdims=True)
        slot = lax.broadcasted_iota(jnp.int32, (tok, capacity), 1).astype(jnp.float32)
        select = jnp.where(slot == position, 1.0, 0.0).astype(jnp.bfloat16)
        to_ref[...] = select
        scaled = (factor * ref[:, :dcols].astype(jnp.float32)).astype(jnp.bfloat16)
        picked.append(lax.dot_general(select, scaled, TN, preferred_element_type=jnp.float32))
    slots = jnp.concatenate(picked, axis=0).astype(jnp.bfloat16)
    every_ref[first * capacity : (first + count) * capacity] = slots
    partial_ref[...] = lax.dot_general(
        slots, wdown_ref[...], NT, preferred_element_type=jnp.float32
    ).astype(jnp.bfloat16)


def take_rows(first, me, wdown, rows, every, total, experts):
    count, tok = len(rows), rows[0].shape[0]
    ff, dcols = wdown.shape
    capacity = total // experts
    smem = pl.BlockSpec(memory_space=pltpu.SMEM)
    old = [] if every is None else [every]
    lead = jax.ShapeDtypeStruct((tok, capacity), jnp.bfloat16)
    return pl.pallas_call(
        functools.partial(take_kernel, experts, count, first),
        in_specs=[smem] + [VMEM] * (1 + count + len(old)),
        out_specs=[VMEM] * (2 + count),
        out_shape=[
            pltpu.VMEM((total, dcols), jnp.bfloat16),
            jax.ShapeDtypeStruct((count * capacity, ff), jnp.bfloat16),
        ]
        + [lead] * count,
        input_output_aliases={2 + count: 0} if old else {},
        compiler_params=pltpu.CompilerParams(vmem_limit_bytes=14 << 20),
        cost_estimate=FREE,
        name="take",
    )(me, wdown, *rows, *old)


def give_kernel(count, first, mine_ref, theirs_ref, to_gate_ref, to_up_ref, wgate_ref, wup_ref, *refs):
    leads, outs = refs[:count], refs[count:]
    capacity = mine_ref.shape[0] // count
    span = slice(first * capacity, (first + count) * capacity)
    dh = mine_ref[...].astype(jnp.float32) + theirs_ref[...].astype(jnp.float32)
    dh = dh.astype(jnp.bfloat16).astype(jnp.float32)

    def scaled(ref):
        return (dh * ref[span].astype(jnp.float32)).astype(jnp.bfloat16)

    slot_grad = lax.dot_general(
        scaled(to_gate_ref), wgate_ref[...], NT, preferred_element_type=jnp.float32
    )
    slot_grad += lax.dot_general(
        scaled(to_up_ref), wup_ref[...], NT, preferred_element_type=jnp.float32
    )
    for i, (lead, out) in enumerate(zip(leads, outs)):
        part = slot_grad[i * capacity : (i + 1) * capacity].astype(jnp.bfloat16)
        out[...] = jnp.dot(lead[...], part, preferred_element_type=jnp.float32).astype(jnp.bfloat16)


def give_rows(first, mine, theirs, to_gate, to_up, wgate, wup, leads):
    count, tok = len(leads), leads[0].shape[0]
    out = jax.ShapeDtypeStruct((tok, wgate.shape[0]), jnp.bfloat16)
    return pl.pallas_call(
        functools.partial(give_kernel, count, first),
        in_specs=[VMEM] * (6 + count),
        out_specs=[VMEM] * count,
        out_shape=[out] * count,
        compiler_params=pltpu.CompilerParams(vmem_limit_bytes=16 << 20),
        cost_estimate=FREE,
        name="give",
    )(mine, theirs, to_gate, to_up, wgate, wup, *leads)


def add_kernel(span, own_ref, given_ref, *refs):
    out_ref = refs[-1]
    total = own_ref[:, span].astype(jnp.float32) + given_ref[:, span].astype(jnp.float32)
    if len(refs) > 1:
        received = jnp.concatenate([ref[...] for ref in refs[:-1]], axis=1)
        if received.shape != total.shape:
            received = received[:, span]
        total += received.astype(jnp.float32)
    out_ref[...] = total.astype(out_ref.dtype)


def add(span, own, given, received):
    parts = (own, given, *received)
    return pl.pallas_call(
        functools.partial(add_kernel, span),
        in_specs=[VMEM] * len(parts),
        out_specs=VMEM,
        out_shape=jax.ShapeDtypeStruct((own.shape[0], span.stop - span.start), own.dtype),
        compiler_params=pltpu.CompilerParams(vmem_limit_bytes=8 << 20),
        cost_estimate=FREE,
        name="add",
    )(*parts)


def grad_kernel(hidden_ref, every_ref, after_ref, *refs):
    refs[-1][...] = jnp.dot(
        hidden_ref[...], every_ref[...], preferred_element_type=jnp.float32
    ).astype(jnp.bfloat16)


def grad_rows(hidden, every, after, part, old):
    (ff, slots), dcols = hidden.shape, every.shape[1]
    rows = ff // 4
    return pl.pallas_call(
        grad_kernel,
        grid=(2,),
        in_specs=[pl.BlockSpec((rows, slots), lambda i: (2 * part + i, 0)), VMEM]
        + [ANY] * (1 + len(old)),
        out_specs=pl.BlockSpec((rows, dcols), lambda i: (2 * part + i, 0)),
        out_shape=jax.ShapeDtypeStruct((ff, dcols), jnp.bfloat16),
        input_output_aliases={3: 0} if old else {},
        compiler_params=pltpu.CompilerParams(vmem_limit_bytes=14 << 20),
        cost_estimate=FREE,
        name="grad_down",
    )(hidden, every, after, *old)


def mark(array, us):
    return pl.pallas_call(
        lambda old_ref, new_ref: None,
        in_specs=[ANY],
        out_specs=ANY,
        out_shape=jax.ShapeDtypeStruct(array.shape, array.dtype),
        input_output_aliases={0: 0},
        compiler_params=pltpu.CompilerParams(vmem_limit_bytes=1 << 20),
        cost_estimate=pl.CostEstimate(
            flops=int(us * 1.1e9), bytes_accessed=int(us * 3.6e6), transcendentals=0
        ),
        name="mark",
    )(array)


def mark(array, us):
    return pl.pallas_call(
        lambda old_ref, new_ref: None,
        in_specs=[ANY],
        out_specs=ANY,
        out_shape=jax.ShapeDtypeStruct(array.shape, array.dtype),
        input_output_aliases={0: 0},
        compiler_params=pltpu.CompilerParams(vmem_limit_bytes=1 << 20),
        cost_estimate=pl.CostEstimate(
            flops=int(us * 1.1e9), bytes_accessed=int(us * 3.6e6), transcendentals=0
        ),
        name="mark",
    )(array)


def sort_kernel(ids_ref, *refs):
    parts, out_ref, done = refs[:-2], refs[-2], refs[-1]
    copies, n = [], 0
    for part in parts:
        for i in range(part.shape[0]):
            copies.append(pltpu.make_async_copy(part.at[i], out_ref.at[ids_ref[n]], done.at[n]))
            n += 1
    for copy in copies:
        copy.start()
    for copy in copies:
        copy.wait()


def sort(ids, parts):
    groups = ids.shape[0]
    return pl.pallas_call(
        sort_kernel,
        in_specs=[pl.BlockSpec(memory_space=pltpu.SMEM)] + [ANY] * len(parts),
        out_specs=ANY,
        out_shape=jax.ShapeDtypeStruct((groups,) + parts[0].shape[1:], jnp.bfloat16),
        scratch_shapes=[pltpu.SemaphoreType.DMA((groups,))],
        compiler_params=pltpu.CompilerParams(vmem_limit_bytes=1 << 20),
        cost_estimate=FREE,
        name="sort",
    )(ids, *parts)


def ring_local(grad_out, routing, gates, scales, saved_gate, saved_up, w_gate, w_up, w_down):
    tok_rows, dcols = grad_out.shape
    groups = lax.axis_size("expert")
    slots = saved_gate.shape[2]
    capacity = slots // groups
    chips = groups // 2
    order = ring_of(chips)
    place = np.argsort(np.array(order))
    after = {order[i]: order[(i + 1) % chips] for i in range(chips)}
    ring = [(2 * j, 2 * after[j]) for j in range(chips)]
    ring += [(2 * after[j] + 1, 2 * j + 1) for j in range(chips)]
    sibling = [(i, i ^ 1) for i in range(groups)]
    swap = [(0, 1), (1, 0)]
    me = lax.axis_index("expert")
    back = [(b, a) for a, b in ring]
    stages = [(s, chips - s) for s in range(1, chips // 2)] + [(chips // 2,)]
    steps = [s for stage in stages for s in stage] + [0]
    table = np.zeros((groups, groups), np.int32)
    for device in range(groups):
        spot = place[device // 2]
        for i, step in enumerate(steps):
            down = 2 * order[(spot - step) % chips]
            up = 2 * order[(spot + step) % chips] + 1
            table[device, 2 * i : 2 * i + 2] = (down, up) if device % 2 == 0 else (up, down)
    ids = lax.dynamic_slice(jnp.asarray(table), (me, 0), (1, groups)).reshape(-1)
    me = me.reshape(1)

    payload = pack(grad_out, routing, gates, scales, groups)
    tiles = -(-saved_gate.shape[1] // LANES)
    wdown, _ = hold(w_down[0], payload, ids)

    tie = lax.optimization_barrier
    rows, others = {0: payload}, {}
    leads, partial, theirs, own, given, totals = {}, {}, {}, {}, {}, {}

    def pass_on(stage):
        for s in stage:
            if s <= chips // 2:
                rows[s] = lax.ppermute(rows[s - 1], "expert", ring)
            else:
                rows[s] = lax.ppermute(rows[(s + 1) % chips], "expert", back)

    def share(stage):
        for s in stage:
            others[s] = lax.ppermute(rows[s], "expert", sibling)

    def take(stage, every=None):
        near_far = [a for s in stage for a in (rows[s], others[s])]
        every, partial[stage], *leads[stage] = take_rows(
            2 * steps.index(stage[0]), me, wdown, near_far, every, slots, groups
        )
        return every

    def trade(stage):
        theirs[stage] = lax.ppermute(partial[stage], "dp", swap)

    def give(stage, marked=False):
        first = 2 * steps.index(stage[0])
        there = theirs[stage] if marked else mark(theirs[stage], 10.0)
        parts = give_rows(
            first, partial[stage], there, to_gate, to_up, *held, leads[stage]
        )
        for i, s in enumerate(stage):
            own[s] = parts[2 * i]
            given[s] = lax.ppermute(parts[2 * i + 1], "expert", sibling)

    def collect(s, before):
        received = [] if before is None else totals[before]
        estimate = 8.0 if s <= HALVES else 1.0
        received = [mark(lax.ppermute(part, "expert", ring), estimate) for part in received]
        if s == HALVES:
            received = [mark(part, 8.0) for part in received]
        pieces = 2 if s >= HALVES else 1
        width = dcols // pieces
        totals[s] = []
        for p in range(pieces):
            mine = received[p : p + 1] if len(received) == pieces else received
            span = slice(p * width, (p + 1) * width)
            totals[s].append(add(span, own[s], given[s], mine))

    def after(values, keys, guard, key):
        *kept, guard[key] = tie(tuple(values[k] for k in keys) + (guard[key],))
        for k, v in zip(keys, kept):
            values[k] = v

    last = (0,)
    pass_on(stages[0])
    share(last)
    every = take(last)
    ids, partial[last] = tie((ids, partial[last]))
    *factors, token = prep(ids, saved_gate[0], saved_up[0], capacity, (0, SPLIT))
    rows[1], early = tie((rows[1], token))
    after(rows, stages[0], partial, last)
    before = last
    for i, stage in enumerate(stages):
        final = i + 1 == len(stages)
        if not final:
            pass_on(stages[i + 1])
        share(stage)
        every = take(stage, every)
        trade(stage)
        if i == 2:
            after(own, [1], partial, stage)
            collect(1, None)
        if i == 0:
            ids, partial[stage] = tie((ids, partial[stage]))
            to_gate, to_up, hidden, token = prep(
                ids, saved_gate[0], saved_up[0], capacity, (SPLIT, tiles), factors
            )
            wgate, token = hold(w_gate[0], early, token)
            tokens = [token]
            after(rows, stages[1], tokens, 0)
        else:
            if i == 1:
                wup, _ = hold(w_up[0], leads[stage][0], *tokens)
                held = (wgate, wup)
            after(theirs, [before], partial, stage)
            give(before)
            if not final:
                after(rows, stages[i + 1], own, before[0])
            if i > 1:
                collect(before[0], before[0] - 1)
        before = stage
    after(theirs, [before], totals[before[0] - 1], 0)
    after(partial, [last], totals[before[0] - 1], 0)
    trade(last)
    give(before)
    for s in range(before[0], chips):
        collect(s, s - 1)
        if s == before[0]:
            grads = [grad_rows(hidden, every, totals[s][1], 0, [])]
            after(given, [s + 1], grads, 0)
        if s == before[0] + 1:
            after(theirs, [last], totals[s], 1)
            give(last)
            after(given, [s + 2], own, 0)
    grads = [grad_rows(hidden, every, totals[chips - 1][0], 1, grads)]
    received = [mark(lax.ppermute(part, "expert", ring), 1.0) for part in totals[chips - 1]]
    grad_x = add(slice(0, dcols), own[0], given[0], received)
    (grad_down,) = grads
    return (grad_x, grad_down[None])


def solution(mesh):
    paired = mesh.shape["dp"] == 2 and mesh.shape["expert"] % 4 == 0
    return jax.shard_map(
        ring_local if paired else exchange_local,
        mesh=mesh,
        in_specs=(
            P("expert", "dp"),
            P("expert", None),
            P("expert", None),
            P("expert"),
            P("expert", None, None),
            P("expert", None, None),
            P("expert", "dp", None),
            P("expert", "dp", None),
            P("expert", None, "dp"),
        ),
        out_specs=(P("expert", "dp"), P("expert", None, "dp")),
        check_vma=False,
    )
```

```python
import functools

import jax
import jax.numpy as jnp
import numpy as np
from jax import lax
from jax.experimental import pallas as pl
from jax.experimental.pallas import tpu as pltpu
from jax.sharding import PartitionSpec as P

LANES = 128
PIECES = 4
HALVES = 4
SPLIT = 6
NT = (((1,), (1,)), ((), ()))
TN = (((0,), (0,)), ((), ()))
VMEM = pl.BlockSpec(memory_space=pltpu.VMEM)
ANY = pl.BlockSpec(memory_space=pl.ANY)
TOKEN = jax.ShapeDtypeStruct((8, LANES), jnp.float32)
FREE = pl.CostEstimate(flops=0, bytes_accessed=0, transcendentals=0)


def activation_grad(hidden_grad, gate_pre, up_pre):
    g = gate_pre.astype(jnp.float32)
    u = up_pre.astype(jnp.float32)
    sig = jax.nn.sigmoid(g)
    dh = hidden_grad.astype(jnp.float32)
    gate_grad = (dh * u * sig * (1.0 + g * (1.0 - sig))).astype(jnp.bfloat16)
    up_grad = (dh * g * sig).astype(jnp.bfloat16)
    return (gate_grad, up_grad)


def contract(left, weights):
    return lax.dot_general(
        left, weights, (((0,), (1,)), ((), ())), preferred_element_type=jnp.float32
    )


def exchange_local(grad_out, routing, gates, scales, saved_gate, saved_up, w_gate, w_up, w_down):
    tok_rows, dcols = grad_out.shape
    topk = routing.shape[1]
    groups = lax.axis_size("expert")
    experts = groups * w_gate.shape[0]
    slots = saved_gate.shape[2]
    capacity = slots // groups
    flat_route = routing.reshape(-1)
    hot = (flat_route[:, None] == jnp.arange(experts, dtype=jnp.int32)[None, :]).astype(jnp.int32)
    position = jnp.sum(hot * (jnp.cumsum(hot, axis=0) - 1), axis=1)
    target = flat_route * capacity + position
    select = jnp.arange(experts * capacity, dtype=jnp.int32)[:, None] == target[None, :]
    weight = (gates * scales[:, None]).reshape(-1)
    slot_factor = jnp.sum(jnp.where(select, weight[None, :], 0.0), axis=1)
    collect = jnp.any(select.reshape(experts * capacity, tok_rows, topk), axis=2).astype(
        jnp.bfloat16
    )
    owned_rows = jnp.dot(collect, grad_out, preferred_element_type=jnp.float32)
    sending = (
        (slot_factor[:, None] * owned_rows).astype(jnp.bfloat16).reshape(experts, capacity, dcols)
    )
    arrived = lax.all_to_all(sending, "expert", split_axis=0, concat_axis=0, tiled=True).reshape(
        slots, dcols
    )
    wdown = w_down[0]
    wgate = w_gate[0]
    wup = w_up[0]
    sgate = saved_gate[0]
    sup = saved_up[0]
    partial_value = lax.dot_general(
        wdown, arrived, (((1,), (1,)), ((), ())), preferred_element_type=jnp.float32
    )
    reduced = lax.psum_scatter(
        partial_value.astype(jnp.bfloat16), "dp", scatter_dimension=0, tiled=True
    )
    hidden_grad = lax.all_gather(reduced, "dp", axis=0, tiled=True)
    gate_grad, up_grad = activation_grad(hidden_grad, sgate, sup)
    slot_grad = contract(gate_grad, wgate) + contract(up_grad, wup)
    gate_full = sgate.astype(jnp.float32)
    hidden = (gate_full * jax.nn.sigmoid(gate_full) * sup.astype(jnp.float32)).astype(jnp.bfloat16)
    grad_down = jnp.dot(hidden, arrived, preferred_element_type=jnp.float32).astype(jnp.bfloat16)
    returning = slot_grad.astype(jnp.bfloat16).reshape(groups, capacity, dcols)
    back = lax.all_to_all(returning, "expert", split_axis=0, concat_axis=0, tiled=True).reshape(
        experts * capacity, dcols
    )
    grad_x = lax.dot_general(
        collect, back, (((0,), (0,)), ((), ())), preferred_element_type=jnp.float32
    )
    return (grad_x.astype(jnp.bfloat16), grad_down[None])


def ring_of(chips):
    return list(range(0, chips, 2)) + list(range(1, chips, 2))[::-1]


def pack_kernel(experts, rows_ref, routing_ref, gates_ref, scales_ref, out_ref):
    topk, tok = routing_ref.shape
    dcols = rows_ref.shape[1]
    lanes = out_ref.shape[1] - dcols
    out_ref[:, :dcols] = rows_ref[...]
    line = lax.broadcasted_iota(jnp.int32, (lanes, tok), 0)
    expert = line % experts
    piece = line // experts
    hot = jnp.zeros((lanes, tok), jnp.float32)
    factor = jnp.zeros((lanes, tok), jnp.float32)
    for k in range(topk):
        same = routing_ref[k : k + 1] == expert
        hot += jnp.where(same, 1.0, 0.0)
        factor += jnp.where(same, gates_ref[k : k + 1] * scales_ref[...], 0.0)
    row = lax.broadcasted_iota(jnp.int32, (tok, tok), 0)
    column = lax.broadcasted_iota(jnp.int32, (tok, tok), 1)
    earlier = jnp.where(row < column, 1.0, 0.0).astype(jnp.bfloat16)
    before = jnp.dot(hot.astype(jnp.bfloat16), earlier, preferred_element_type=jnp.float32)
    high = factor.astype(jnp.bfloat16)
    rest = factor - high.astype(jnp.float32)
    middle = rest.astype(jnp.bfloat16)
    low = rest - middle.astype(jnp.float32)
    meta = jnp.where(piece == 0, hot * (before + 1.0), 0.0)
    meta = jnp.where(piece == 1, high.astype(jnp.float32), meta)
    meta = jnp.where(piece == 2, middle.astype(jnp.float32), meta)
    meta = jnp.where(piece == 3, low, meta)
    out_ref[:, dcols:] = meta.T.astype(jnp.bfloat16)


def whole(shape):
    return pl.BlockSpec(shape, lambda i: (0,) * len(shape))


def pack(rows, routing, gates, scales, experts):
    tok, dcols = rows.shape
    lanes = -(-PIECES * experts // LANES) * LANES
    operands = [
        pltpu.with_memory_space_constraint(a, pltpu.HBM)
        for a in (rows, routing.T, gates.T, scales[None])
    ]
    return pl.pallas_call(
        functools.partial(pack_kernel, experts),
        grid=(1,),
        in_specs=[whole(a.shape) for a in operands],
        out_specs=whole((tok, dcols + lanes)),
        out_shape=jax.ShapeDtypeStruct((tok, dcols + lanes), jnp.bfloat16),
        compiler_params=pltpu.CompilerParams(vmem_limit_bytes=8 << 20),
        cost_estimate=FREE,
        name="pack",
    )(*operands)


def prep_kernel(capacity, first, ids_ref, gate_ref, up_ref, *refs):
    to_gate_ref, to_up_ref, hidden_ref, token_ref, turned = refs[-5:]
    g = gate_ref[...].astype(jnp.float32)
    u = up_ref[...].astype(jnp.float32)
    sig = jax.nn.sigmoid(g)
    swish = g * sig
    turned[0] = (u * sig * (1.0 + g * (1.0 - sig))).T
    turned[1] = swish.T
    turned[2] = (swish * u).T

    def in_order(k):
        groups = gate_ref.shape[1] // capacity
        starts = [pl.multiple_of(ids_ref[i] * capacity, 8) for i in range(groups)]
        return jnp.concatenate([turned[k, pl.ds(start, capacity)] for start in starts], axis=0)

    span = pl.ds(pl.multiple_of((first + pl.program_id(0)) * LANES, LANES), LANES)
    to_gate_ref[:, span] = in_order(0).astype(jnp.bfloat16)
    to_up_ref[:, span] = in_order(1).astype(jnp.bfloat16)
    hidden_ref[span] = in_order(2).T.astype(jnp.bfloat16)
    token_ref[...] = jnp.zeros(token_ref.shape, token_ref.dtype)


def prep(ids, gate, up, capacity, tiles, old=()):
    ff, slots = gate.shape
    spec = pl.BlockSpec((LANES, slots), lambda i, ids: (tiles[0] + i, 0))
    operands = [pltpu.with_memory_space_constraint(a, pltpu.HBM) for a in (gate, up)]
    count = (tiles[1] - tiles[0]) * LANES
    return pl.pallas_call(
        functools.partial(prep_kernel, capacity, tiles[0]),
        grid_spec=pltpu.PrefetchScalarGridSpec(
            num_scalar_prefetch=1,
            grid=(tiles[1] - tiles[0],),
            in_specs=[spec, spec] + [VMEM] * len(old),
            out_specs=[VMEM] * 3 + [pl.BlockSpec(TOKEN.shape, lambda i, ids: (0, 0))],
            scratch_shapes=[pltpu.VMEM((3, slots, LANES), jnp.float32)],
        ),
        out_shape=[
            pltpu.VMEM((slots, ff), jnp.bfloat16),
            pltpu.VMEM((slots, ff), jnp.bfloat16),
            pltpu.VMEM((ff, slots), jnp.bfloat16),
            TOKEN,
        ],
        input_output_aliases={3 + i: i for i in range(len(old))},
        compiler_params=pltpu.CompilerParams(vmem_limit_bytes=8 << 20),
        cost_estimate=pl.CostEstimate(
            flops=10 * count * slots, bytes_accessed=10 * count * slots, transcendentals=count * slots
        ),
        name="prep",
    )(ids, *operands, *old)


def hold_kernel(weights_ref, *refs):
    out_ref, token_ref, done = refs[-3:]
    copy = pltpu.make_async_copy(weights_ref, out_ref, done)
    copy.start()
    token_ref[...] = jnp.zeros(token_ref.shape, token_ref.dtype)
    copy.wait()


def hold(weights, *after):
    return pl.pallas_call(
        hold_kernel,
        in_specs=[ANY] * (1 + len(after)),
        out_specs=[VMEM, VMEM],
        out_shape=[pltpu.VMEM(weights.shape, weights.dtype), TOKEN],
        scratch_shapes=[pltpu.SemaphoreType.DMA(())],
        compiler_params=pltpu.CompilerParams(vmem_limit_bytes=1 << 20),
        cost_estimate=FREE,
        name="hold",
    )(pltpu.with_memory_space_constraint(weights, pltpu.HBM), *after)


def take_kernel(experts, count, first, me_ref, wdown_ref, *refs):
    rows, (every_ref, partial_ref, *leads) = refs[:count], refs[-2 - count :]
    dcols = every_ref.shape[1]
    capacity = every_ref.shape[0] // experts
    me = me_ref[0]
    picked = []
    for ref, to_ref in zip(rows, leads):
        meta = ref[:, dcols:].astype(jnp.float32)
        tok, lanes = meta.shape
        lane = lax.broadcasted_iota(jnp.int32, (tok, lanes), 1)
        mine = lane % experts == me
        places = jnp.where(mine & (lane < experts), meta, 0.0)
        share = jnp.where(mine & (lane >= experts), meta, 0.0)
        position = jnp.sum(places, axis=1, keepdims=True) - 1.0
        factor = jnp.sum(share, axis=1, keepdims=True)
        slot = lax.broadcasted_iota(jnp.int32, (tok, capacity), 1).astype(jnp.float32)
        select = jnp.where(slot == position, 1.0, 0.0).astype(jnp.bfloat16)
        to_ref[...] = select
        scaled = (factor * ref[:, :dcols].astype(jnp.float32)).astype(jnp.bfloat16)
        picked.append(lax.dot_general(select, scaled, TN, preferred_element_type=jnp.float32))
    slots = jnp.concatenate(picked, axis=0).astype(jnp.bfloat16)
    every_ref[first * capacity : (first + count) * capacity] = slots
    partial_ref[...] = lax.dot_general(
        slots, wdown_ref[...], NT, preferred_element_type=jnp.float32
    ).astype(jnp.bfloat16)


def take_rows(first, me, wdown, rows, every, total, experts):
    count, tok = len(rows), rows[0].shape[0]
    ff, dcols = wdown.shape
    capacity = total // experts
    smem = pl.BlockSpec(memory_space=pltpu.SMEM)
    old = [] if every is None else [every]
    lead = jax.ShapeDtypeStruct((tok, capacity), jnp.bfloat16)
    return pl.pallas_call(
        functools.partial(take_kernel, experts, count, first),
        in_specs=[smem] + [VMEM] * (1 + count + len(old)),
        out_specs=[VMEM] * (2 + count),
        out_shape=[
            pltpu.VMEM((total, dcols), jnp.bfloat16),
            jax.ShapeDtypeStruct((count * capacity, ff), jnp.bfloat16),
        ]
        + [lead] * count,
        input_output_aliases={2 + count: 0} if old else {},
        compiler_params=pltpu.CompilerParams(vmem_limit_bytes=14 << 20),
        cost_estimate=FREE,
        name="take",
    )(me, wdown, *rows, *old)


def give_kernel(count, first, mine_ref, theirs_ref, to_gate_ref, to_up_ref, wgate_ref, wup_ref, *refs):
    leads, outs = refs[:count], refs[count:]
    capacity = mine_ref.shape[0] // count
    span = slice(first * capacity, (first + count) * capacity)
    dh = mine_ref[...].astype(jnp.float32) + theirs_ref[...].astype(jnp.float32)
    dh = dh.astype(jnp.bfloat16).astype(jnp.float32)

    def scaled(ref):
        return (dh * ref[span].astype(jnp.float32)).astype(jnp.bfloat16)

    slot_grad = lax.dot_general(
        scaled(to_gate_ref), wgate_ref[...], NT, preferred_element_type=jnp.float32
    )
    slot_grad += lax.dot_general(
        scaled(to_up_ref), wup_ref[...], NT, preferred_element_type=jnp.float32
    )
    for i, (lead, out) in enumerate(zip(leads, outs)):
        part = slot_grad[i * capacity : (i + 1) * capacity].astype(jnp.bfloat16)
        out[...] = jnp.dot(lead[...], part, preferred_element_type=jnp.float32).astype(jnp.bfloat16)


def give_rows(first, mine, theirs, to_gate, to_up, wgate, wup, leads):
    count, tok = len(leads), leads[0].shape[0]
    out = jax.ShapeDtypeStruct((tok, wgate.shape[0]), jnp.bfloat16)
    return pl.pallas_call(
        functools.partial(give_kernel, count, first),
        in_specs=[VMEM] * (6 + count),
        out_specs=[VMEM] * count,
        out_shape=[out] * count,
        compiler_params=pltpu.CompilerParams(vmem_limit_bytes=16 << 20),
        cost_estimate=FREE,
        name="give",
    )(mine, theirs, to_gate, to_up, wgate, wup, *leads)


def add_kernel(span, own_ref, given_ref, *refs):
    out_ref = refs[-1]
    total = own_ref[:, span].astype(jnp.float32) + given_ref[:, span].astype(jnp.float32)
    if len(refs) > 1:
        received = jnp.concatenate([ref[...] for ref in refs[:-1]], axis=1)
        if received.shape != total.shape:
            received = received[:, span]
        total += received.astype(jnp.float32)
    out_ref[...] = total.astype(out_ref.dtype)


def add(span, own, given, received):
    parts = (own, given, *received)
    return pl.pallas_call(
        functools.partial(add_kernel, span),
        in_specs=[VMEM] * len(parts),
        out_specs=VMEM,
        out_shape=jax.ShapeDtypeStruct((own.shape[0], span.stop - span.start), own.dtype),
        compiler_params=pltpu.CompilerParams(vmem_limit_bytes=8 << 20),
        cost_estimate=FREE,
        name="add",
    )(*parts)


def grad_kernel(hidden_ref, every_ref, after_ref, *refs):
    refs[-1][...] = jnp.dot(
        hidden_ref[...], every_ref[...], preferred_element_type=jnp.float32
    ).astype(jnp.bfloat16)


def grad_rows(hidden, every, after, part, old):
    (ff, slots), dcols = hidden.shape, every.shape[1]
    rows = ff // 4
    return pl.pallas_call(
        grad_kernel,
        grid=(2,),
        in_specs=[pl.BlockSpec((rows, slots), lambda i: (2 * part + i, 0)), VMEM]
        + [ANY] * (1 + len(old)),
        out_specs=pl.BlockSpec((rows, dcols), lambda i: (2 * part + i, 0)),
        out_shape=jax.ShapeDtypeStruct((ff, dcols), jnp.bfloat16),
        input_output_aliases={3: 0} if old else {},
        compiler_params=pltpu.CompilerParams(vmem_limit_bytes=14 << 20),
        cost_estimate=FREE,
        name="grad_down",
    )(hidden, every, after, *old)


def mark(array, us):
    return pl.pallas_call(
        lambda old_ref, new_ref: None,
        in_specs=[ANY],
        out_specs=ANY,
        out_shape=jax.ShapeDtypeStruct(array.shape, array.dtype),
        input_output_aliases={0: 0},
        compiler_params=pltpu.CompilerParams(vmem_limit_bytes=1 << 20),
        cost_estimate=pl.CostEstimate(
            flops=int(us * 1.1e9), bytes_accessed=int(us * 3.6e6), transcendentals=0
        ),
        name="mark",
    )(array)


def mark(array, us):
    return pl.pallas_call(
        lambda old_ref, new_ref: None,
        in_specs=[ANY],
        out_specs=ANY,
        out_shape=jax.ShapeDtypeStruct(array.shape, array.dtype),
        input_output_aliases={0: 0},
        compiler_params=pltpu.CompilerParams(vmem_limit_bytes=1 << 20),
        cost_estimate=pl.CostEstimate(
            flops=int(us * 1.1e9), bytes_accessed=int(us * 3.6e6), transcendentals=0
        ),
        name="mark",
    )(array)


def sort_kernel(ids_ref, *refs):
    parts, out_ref, done = refs[:-2], refs[-2], refs[-1]
    copies, n = [], 0
    for part in parts:
        for i in range(part.shape[0]):
            copies.append(pltpu.make_async_copy(part.at[i], out_ref.at[ids_ref[n]], done.at[n]))
            n += 1
    for copy in copies:
        copy.start()
    for copy in copies:
        copy.wait()


def sort(ids, parts):
    groups = ids.shape[0]
    return pl.pallas_call(
        sort_kernel,
        in_specs=[pl.BlockSpec(memory_space=pltpu.SMEM)] + [ANY] * len(parts),
        out_specs=ANY,
        out_shape=jax.ShapeDtypeStruct((groups,) + parts[0].shape[1:], jnp.bfloat16),
        scratch_shapes=[pltpu.SemaphoreType.DMA((groups,))],
        compiler_params=pltpu.CompilerParams(vmem_limit_bytes=1 << 20),
        cost_estimate=FREE,
        name="sort",
    )(ids, *parts)


def ring_local(grad_out, routing, gates, scales, saved_gate, saved_up, w_gate, w_up, w_down):
    tok_rows, dcols = grad_out.shape
    groups = lax.axis_size("expert")
    slots = saved_gate.shape[2]
    capacity = slots // groups
    chips = groups // 2
    order = ring_of(chips)
    place = np.argsort(np.array(order))
    after = {order[i]: order[(i + 1) % chips] for i in range(chips)}
    ring = [(2 * j, 2 * after[j]) for j in range(chips)]
    ring += [(2 * after[j] + 1, 2 * j + 1) for j in range(chips)]
    sibling = [(i, i ^ 1) for i in range(groups)]
    swap = [(0, 1), (1, 0)]
    me = lax.axis_index("expert")
    back = [(b, a) for a, b in ring]
    stages = [(s, chips - s) for s in range(1, chips // 2)] + [(chips // 2,)]
    steps = [s for stage in stages for s in stage] + [0]
    table = np.zeros((groups, groups), np.int32)
    for device in range(groups):
        spot = place[device // 2]
        for i, step in enumerate(steps):
            down = 2 * order[(spot - step) % chips]
            up = 2 * order[(spot + step) % chips] + 1
            table[device, 2 * i : 2 * i + 2] = (down, up) if device % 2 == 0 else (up, down)
    ids = lax.dynamic_slice(jnp.asarray(table), (me, 0), (1, groups)).reshape(-1)
    me = me.reshape(1)

    payload = pack(grad_out, routing, gates, scales, groups)
    tiles = -(-saved_gate.shape[1] // LANES)
    wdown, _ = hold(w_down[0], payload, ids)

    tie = lax.optimization_barrier
    rows, others = {0: payload}, {}
    leads, partial, theirs, own, given, totals = {}, {}, {}, {}, {}, {}

    def pass_on(stage):
        for s in stage:
            if s <= chips // 2:
                rows[s] = lax.ppermute(rows[s - 1], "expert", ring)
            else:
                rows[s] = lax.ppermute(rows[(s + 1) % chips], "expert", back)

    def share(stage):
        for s in stage:
            others[s] = lax.ppermute(rows[s], "expert", sibling)

    def take(stage, every=None):
        near_far = [a for s in stage for a in (rows[s], others[s])]
        every, partial[stage], *leads[stage] = take_rows(
            2 * steps.index(stage[0]), me, wdown, near_far, every, slots, groups
        )
        return every

    def trade(stage):
        theirs[stage] = lax.ppermute(partial[stage], "dp", swap)

    def give(stage, marked=False):
        first = 2 * steps.index(stage[0])
        there = theirs[stage] if marked else mark(theirs[stage], 10.0)
        parts = give_rows(
            first, partial[stage], there, to_gate, to_up, *held, leads[stage]
        )
        for i, s in enumerate(stage):
            own[s] = parts[2 * i]
            given[s] = lax.ppermute(parts[2 * i + 1], "expert", sibling)

    def collect(s, before):
        received = [] if before is None else totals[before]
        estimate = 8.0 if s <= HALVES else 1.0
        received = [mark(lax.ppermute(part, "expert", ring), estimate) for part in received]
        if s == HALVES:
            received = [mark(part, 8.0) for part in received]
        pieces = 2 if s >= HALVES else 1
        width = dcols // pieces
        totals[s] = []
        for p in range(pieces):
            mine = received[p : p + 1] if len(received) == pieces else received
            span = slice(p * width, (p + 1) * width)
            totals[s].append(add(span, own[s], given[s], mine))

    def after(values, keys, guard, key):
        *kept, guard[key] = tie(tuple(values[k] for k in keys) + (guard[key],))
        for k, v in zip(keys, kept):
            values[k] = v

    last = (0,)
    pass_on(stages[0])
    rows[0], ids = tie((rows[0], ids))
    share(last)
    every = take(last)
    ids, partial[last] = tie((ids, partial[last]))
    *factors, token = prep(ids, saved_gate[0], saved_up[0], capacity, (0, SPLIT))
    rows[1], early = tie((rows[1], token))
    after(rows, stages[0], partial, last)
    before = last
    for i, stage in enumerate(stages):
        final = i + 1 == len(stages)
        if not final:
            pass_on(stages[i + 1])
        share(stage)
        every = take(stage, every)
        trade(stage)
        if i == 2:
            after(own, [1], partial, stage)
            collect(1, None)
        if i == 0:
            ids, partial[stage] = tie((ids, partial[stage]))
            to_gate, to_up, hidden, token = prep(
                ids, saved_gate[0], saved_up[0], capacity, (SPLIT, tiles), factors
            )
            wgate, token = hold(w_gate[0], early, token)
            tokens = [token]
            after(rows, stages[1], tokens, 0)
        else:
            if i == 1:
                wup, _ = hold(w_up[0], leads[stage][0], *tokens)
                held = (wgate, wup)
            after(theirs, [before], partial, stage)
            give(before)
            if not final:
                after(rows, stages[i + 1], own, before[0])
            if i > 1:
                collect(before[0], before[0] - 1)
        before = stage
    after(theirs, [before], totals[before[0] - 1], 0)
    after(partial, [last], totals[before[0] - 1], 0)
    trade(last)
    give(before)
    for s in range(before[0], chips):
        collect(s, s - 1)
        if s == before[0]:
            grads = [grad_rows(hidden, every, totals[s][1], 0, [])]
            after(given, [s + 1], grads, 0)
        if s == before[0] + 1:
            after(theirs, [last], totals[s], 1)
            give(last)
            after(given, [s + 2], own, 0)
    grads = [grad_rows(hidden, every, totals[chips - 1][0], 1, grads)]
    received = [mark(lax.ppermute(part, "expert", ring), 1.0) for part in totals[chips - 1]]
    grad_x = add(slice(0, dcols), own[0], given[0], received)
    (grad_down,) = grads
    return (grad_x, grad_down[None])


def solution(mesh):
    paired = mesh.shape["dp"] == 2 and mesh.shape["expert"] % 4 == 0
    return jax.shard_map(
        ring_local if paired else exchange_local,
        mesh=mesh,
        in_specs=(
            P("expert", "dp"),
            P("expert", None),
            P("expert", None),
            P("expert"),
            P("expert", None, None),
            P("expert", None, None),
            P("expert", "dp", None),
            P("expert", "dp", None),
            P("expert", None, "dp"),
        ),
        out_specs=(P("expert", "dp"), P("expert", None, "dp")),
        check_vma=False,
    )
```
